32 devices in a mesh: seq: 8 (over z, core), dp: 4 (over y, x).
Axes of the slice: x: 2, y: 2, z: 4, core: 2. Of those that a mesh axis runs over, the one named last changes fastest.
Arguments:
- skip_input: bfloat16 [8, 2048, 768], P('dp', 'seq'), may hold values from -6 to 6
- upstream: bfloat16 [8, 2048, 1280], P('dp', 'seq'), may hold values from -6 to 6
- proj_weight: bfloat16 [768, 1280], replicated, may hold values from -0.21875 to 0.21875
- depth_kernel: float32 [3, 1280], replicated, may hold values from -3 to 3
Outputs:
- input_grad: bfloat16 [8, 2048, 768], P('dp', 'seq')
- weight_grad: float32 [768, 1280], P('dp', 'seq')
The draws below stay inside these ranges and needn't reach their ends.
All inputs are finite; a program needn't handle non-finite values.
Results may differ from the reference program's by a relative error of at most 0.0053.
Values may be sent and summed in bfloat16 or wider, within the bound.
No kernel may reach another device: no remote copies, remote signals or barrier semaphores. Data moves between devices by JAX's collectives and lax.ppermute only.
A program may use at most 64 MiB of HBM per device.

```python
import jax
import jax.numpy as jnp
from jax import lax

C = 768
F = 1280
KSIZE = 3
SAMPLES = 8
L = 2048


def levels(rng, dims, cuts, low, high):
    gain, own = 1.0, jax.random.fold_in(rng, 6)
    for dim, shards_of in cuts:
        steps = jnp.exp(jax.random.uniform(jax.random.fold_in(own, dim), (shards_of,), jnp.float32, low / len(cuts), high / len(cuts)))
        gain = gain * jnp.repeat(steps, dims[dim] // shards_of).reshape([-1 if axis == dim else 1 for axis in range(len(dims))])
    return gain


def centred(key, extent, width, limit, split=(), held_as=jnp.bfloat16):
    values = jax.random.normal(key, extent, jnp.float32) * width
    if len(split) > 0:
        values = levels(key, extent, split, -0.22, 0.18) * values
    return jnp.clip(values, min=-limit, max=limit).astype(held_as)


def setup_inputs(seed: int = 0) -> dict:
    seeds = jax.random.split(jax.random.key(seed), 5)
    return {
        "skip_input": centred(seeds[0], (SAMPLES, L, C), 1.0, 6.0, ((0, 4), (1, 8))),
        "upstream": centred(seeds[1], (SAMPLES, L, F), 1.0, 6.0, ((0, 4), (1, 8))),
        "proj_weight": centred(seeds[2], (C, F), C ** -0.5, 0.21875),
        "depth_kernel": centred(seeds[3], (KSIZE, F), 0.6, 3.0, (), jnp.float32),
    }


def gelu_slope(pre, scaled):
    return jax.vjp(jax.nn.gelu, pre)[1](scaled)[0]

def reference(skip_input, upstream, proj_weight, depth_kernel):
    k_left = depth_kernel[0]
    k_mid = depth_kernel[1]
    k_right = depth_kernel[2]

    def per_sample(summed, sample):
        inputs_one, upstream_one = sample
        proj = jnp.dot(inputs_one, proj_weight, preferred_element_type=jnp.float32).astype(jnp.bfloat16)
        proj_f32 = proj.astype(jnp.float32)
        zero_row = jnp.zeros((1, proj_f32.shape[1]), jnp.float32)
        before = jnp.concatenate([zero_row, proj_f32[:-1]], axis=0)
        after = jnp.concatenate([proj_f32[1:], zero_row], axis=0)
        halved = 0.5 * upstream_one.astype(jnp.float32)
        slope_fwd = gelu_slope(k_left * before + k_mid * proj_f32 + k_right * after, halved)
        slope_rev = gelu_slope(k_right * before + k_mid * proj_f32 + k_left * after, halved)
        fwd_before = jnp.concatenate([zero_row, slope_fwd[:-1]], axis=0)
        fwd_after = jnp.concatenate([slope_fwd[1:], zero_row], axis=0)
        rev_before = jnp.concatenate([zero_row, slope_rev[:-1]], axis=0)
        rev_after = jnp.concatenate([slope_rev[1:], zero_row], axis=0)
        grad_proj = (k_left * (fwd_after + rev_before) + k_mid * (slope_fwd + slope_rev) + k_right * (fwd_before + rev_after)).astype(jnp.bfloat16)
        grad_in = jnp.dot(grad_proj, proj_weight.T, preferred_element_type=jnp.float32).astype(jnp.bfloat16)
        partial_value = jnp.dot(inputs_one.T, grad_proj, preferred_element_type=jnp.float32)
        return (summed + partial_value, grad_in)
    start = jnp.zeros((skip_input.shape[2], proj_weight.shape[1]), jnp.float32)
    summed, input_grad = lax.scan(per_sample, start, (skip_input, upstream))
    return (input_grad, summed / SAMPLES)
```

```python
import functools
import math

import jax
import jax.numpy as jnp
from jax import lax
from jax.experimental import pallas as pl
from jax.experimental.pallas import tpu as pltpu
from jax.sharding import PartitionSpec as P

BF16 = jnp.bfloat16
F32 = jnp.float32
C0 = math.sqrt(2.0 / math.pi)
ALPHA = (0.044715 * C0) ** (1.0 / 3.0)
KAPPA = C0 / ALPHA
LANES = 128
SUB = 8
PAD = 8
VMEM_BYTES = 48 * 1024 * 1024


def vmem(count):
    return [pl.BlockSpec(memory_space=pltpu.VMEM)] * count


def smem():
    return [pl.BlockSpec(memory_space=pltpu.SMEM)]


def params():
    return pltpu.CompilerParams(vmem_limit_bytes=VMEM_BYTES)


def shape(dims, dtype):
    return jax.ShapeDtypeStruct(dims, dtype)


def edges_kernel(where_ref, x_ref, u_ref, pair_ref, far_ref, x_low, x_high, u_low, u_high, sems):
    batch, rows, chans = x_ref.shape
    copies = []
    for i, (src, low, high) in enumerate(((x_ref, x_low, x_high), (u_ref, u_low, u_high))):
        copies.append(pltpu.make_async_copy(src.at[:, pl.ds(0, 16), :], low, sems.at[2 * i]))
        copies.append(pltpu.make_async_copy(src.at[:, pl.ds(rows - 16, 16), :], high, sems.at[2 * i + 1]))
    for copy in copies:
        copy.start()
    for copy in copies:
        copy.wait()
    even = where_ref[0] == 0
    for low, high, lo, hi in ((x_low, x_high, 0, chans), (u_low, u_high, chans, pair_ref.shape[1])):
        first = jnp.concatenate([low[b].astype(F32)[:2] for b in range(batch)], axis=0)
        final = jnp.concatenate([high[b].astype(F32)[14:] for b in range(batch)], axis=0)
        pair_ref[:, lo:hi] = jnp.where(even, final, first).astype(BF16)
        far_ref[:, lo:hi] = jnp.where(even, first, final).astype(BF16)


def edges(where, x, u):
    batch, _, chans = x.shape
    feats = u.shape[2]
    return pl.pallas_call(
        edges_kernel,
        out_shape=[shape((2 * batch, chans + feats), BF16)] * 2,
        in_specs=smem() + [pl.BlockSpec(memory_space=pltpu.HBM)] * 2,
        out_specs=vmem(2),
        scratch_shapes=[pltpu.VMEM((batch, 16, chans), BF16)] * 2 + [pltpu.VMEM((batch, 16, feats), BF16)] * 2
        + [pltpu.SemaphoreType.DMA((4,))],
        compiler_params=params(),
        cost_estimate=pl.CostEstimate(flops=10_000_000_000, bytes_accessed=1_000_000, transcendentals=0),
        name="edges",
    )(where, x, u)


def odd_slope(w):
    w2 = w * w
    t = jnp.tanh(w * (w2 + KAPPA))
    return t + w * (w2 + KAPPA / 3.0) * (3.0 - 3.0 * (t * t))


def tap_sets(taps):
    k_sum, k_dif, k_mid = 0.5 * (taps[0:1] + taps[2:3]), 0.5 * (taps[0:1] - taps[2:3]), taps[1:2]
    return (ALPHA * k_sum, ALPHA * k_dif, ALPHA * k_mid), (0.25 * k_sum, 0.25 * k_dif, 0.25 * k_mid)


def slopes(scaled, before, centre, after, u):
    p_sum, p_dif, p_mid = scaled
    same = p_mid * centre + p_sum * (before + after)
    skew = p_dif * (before - after)
    fwd, rev = odd_slope(same + skew), odd_slope(same - skew)
    return u * (2.0 + (fwd + rev)), u * (fwd - rev)


def inner_gradients(j, proj, u_ref, k_ref, wide, out, gp_ref, gp_lane):
    batch, rows = u_ref.shape[:2]
    seg = rows // SUB
    pitch = proj.shape[2] // SUB
    lanes = slice(j * LANES, (j + 1) * LANES)
    scaled, (g_sum, g_dif, g_mid) = tap_sets(k_ref[:, lanes])
    for b in range(batch):
        for s in range(SUB):
            wide[b, s * pitch:s * pitch + seg] = u_ref[b, s * seg:(s + 1) * seg, lanes].astype(F32)
    for b in range(batch):
        def vector(i, b=b):
            return proj[j, b, pl.ds(i, SUB, stride=pitch), :]

        def put(i, before, centre, after, dif_before, dif_after, b=b):
            out[b, pl.ds(i, SUB, stride=pitch), :] = (
                g_mid * centre + g_sum * (before + after) + g_dif * (dif_after - dif_before))

        head, tail = vector(0), vector(seg - 1)
        before, stop = pltpu.roll(tail, 1, 0), pltpu.roll(head, SUB - 1, 0)
        sums, difs = [], []
        centre = head
        for i in range(seg):
            after = stop if i == seg - 1 else (tail if i == seg - 2 else vector(i + 1))
            one, two = slopes(scaled, before, centre, after, wide[b, pl.ds(i, SUB, stride=pitch), :])
            sums.append(one)
            difs.append(two)
            before, centre = centre, after
            if i >= 2:
                put(i - 1, sums[i - 2], sums[i - 1], sums[i], difs[i - 2], difs[i])
        put(0, pltpu.roll(sums[-1], 1, 0), sums[0], sums[1], pltpu.roll(difs[-1], 1, 0), difs[1])
        put(seg - 1, sums[-2], sums[-1], pltpu.roll(sums[0], SUB - 1, 0), difs[-2], pltpu.roll(difs[0], SUB - 1, 0))
        done = jnp.concatenate([out[b, s * pitch:s * pitch + seg] for s in range(SUB)], axis=0)
        gp_ref[b, :, gp_lane:gp_lane + LANES] = done.astype(BF16)


def project_kernel(x_ref, w_ref, u_ref, k_ref, proj, gp_ref, wide, out):
    batch, rows, _ = x_ref.shape
    seg = rows // SUB
    pitch = proj.shape[2] // SUB
    tiles = gp_ref.shape[2] // LANES
    for b in range(batch):
        body = jnp.dot(x_ref[b], w_ref[...], preferred_element_type=F32).astype(BF16).astype(F32)
        for j in range(proj.shape[0]):
            for s in range(SUB):
                proj[j, b, s * pitch:s * pitch + seg] = body[s * seg:(s + 1) * seg, j * LANES:(j + 1) * LANES]
    for j in range(tiles):
        inner_gradients(j, proj, u_ref, k_ref, wide, out, gp_ref, j * LANES)


def sample_scratch(batch, rows):
    return [pltpu.VMEM((batch, rows + SUB * PAD, LANES), F32)] * 2


def project(x, w, u, k, ncol):
    batch, rows, _ = x.shape
    feats = w.shape[1]
    return pl.pallas_call(
        project_kernel,
        out_shape=[shape((feats // LANES, batch, rows + SUB * PAD, LANES), F32), shape((batch, rows, ncol), BF16)],
        in_specs=vmem(4),
        out_specs=vmem(2),
        scratch_shapes=sample_scratch(batch, rows),
        compiler_params=params(),
        cost_estimate=pl.CostEstimate(flops=4_000_000_000, bytes_accessed=4_000_000, transcendentals=0),
        name="project",
    )(x, w, u, k)


def around(low, high):
    return jnp.concatenate([low, jnp.zeros((SUB - 4, low.shape[1]), low.dtype), high], axis=0)


def halo_of(where_ref, pair_ref, far_ref, lo, hi, batch):
    even = where_ref[0] == 0
    pair, far = pair_ref[:, lo:hi].astype(F32), far_ref[:, lo:hi].astype(F32)
    low, high = jnp.where(even, far, pair), jnp.where(even, pair, far)
    return [around(low[2 * b:2 * b + 2], high[2 * b:2 * b + 2]) for b in range(batch)]


def finish(j, proj, u_ref, k_ref, halo_p, halo_u, inner_ref, gp_ref, gp_lane, gpt):
    batch, rows = u_ref.shape[:2]
    pitch = proj.shape[2] // SUB
    seg = rows // SUB
    lanes = slice(j * LANES, (j + 1) * LANES)
    cols = slice(gp_lane, gp_lane + LANES)
    scaled, (g_sum, g_dif, g_mid) = tap_sets(k_ref[:, lanes])
    sub = lax.broadcasted_iota(jnp.int32, (SUB, LANES), 0)

    def centred(low, high, halo):
        ends = jnp.where(sub == 0, pltpu.roll(halo, SUB - 1, 0), pltpu.roll(halo, 1, 0))
        inside = jnp.where(sub < 4, pltpu.roll(low, 1, 0), pltpu.roll(high, SUB - 1, 0))
        return jnp.where(jnp.logical_or(sub == 0, sub == SUB - 1), ends, inside)

    for b in range(batch):
        low = proj[j, b, 0:SUB]
        high = proj[j, b, (SUB - 1) * pitch + seg - SUB:(SUB - 1) * pitch + seg]
        halo = halo_p[b][:, lanes]
        before = jnp.where(sub < 2, halo, jnp.where(sub < 4, pltpu.roll(low, 2, 0), high))
        after = jnp.where(sub < 4, low, jnp.where(sub < 6, pltpu.roll(high, SUB - 2, 0), halo))
        u_low = u_ref[b, 0:16, lanes].astype(F32)[:SUB]
        u_high = u_ref[b, rows - 16:rows, lanes].astype(F32)[16 - SUB:]
        u = centred(u_low, u_high, halo_u[b][:, lanes])
        sums, difs = slopes(scaled, before, centred(low, high, halo), after, u)
        ends = (g_mid * sums + g_sum * (pltpu.roll(sums, 1, 0) + pltpu.roll(sums, SUB - 1, 0))
                + g_dif * (pltpu.roll(difs, SUB - 1, 0) - pltpu.roll(difs, 1, 0)))
        first = inner_ref[b, 0:16, cols].astype(F32)
        last_rows = inner_ref[b, rows - 16:rows, cols].astype(F32)
        first = jnp.concatenate([jnp.where(sub < 2, pltpu.roll(ends, SUB - 1, 0), first[:SUB]), first[SUB:]], axis=0)
        last_rows = jnp.concatenate(
            [last_rows[:SUB], jnp.where(sub >= 6, pltpu.roll(ends, 1, 0), last_rows[SUB:])], axis=0)
        gp_ref[b, 0:16, cols] = first.astype(BF16)
        gp_ref[b, rows - 16:rows, cols] = last_rows.astype(BF16)
        if inner_ref is not gp_ref:
            gp_ref[b, 16:rows - 16, cols] = inner_ref[b, 16:rows - 16, cols]
        gpt[cols, b * rows:(b + 1) * rows] = gp_ref[b, :, cols].T


def hand_out(core, gpt, mine_ref, send_ref):
    strip = mine_ref.shape[1]
    for z in range(mine_ref.shape[0]):
        for result, who in ((mine_ref, core), (send_ref, 1 - core)):
            result[z] = gpt[pl.ds(pl.multiple_of((2 * z + who) * strip, 16), strip), :]


def early_kernel(
    where_ref, x_ref, w_ref, u_ref, k_ref, pair_ref, far_ref, proj, inner_ref,
    gp_ref, halo_ref, *rest,
):
    *parts, gpt = rest
    batch, rows, chans = x_ref.shape
    halo_x = halo_of(where_ref, pair_ref, far_ref, 0, chans, batch)
    halo_u = halo_of(where_ref, pair_ref, far_ref, chans, pair_ref.shape[1], batch)
    halo_x = jnp.concatenate(halo_x, axis=0).astype(BF16)
    halo_all = jnp.dot(halo_x, w_ref[...], preferred_element_type=F32).astype(BF16).astype(F32)
    for b in range(batch):
        halo_ref[b] = halo_all[b * SUB:(b + 1) * SUB]
    halo_p = [halo_all[b * SUB:(b + 1) * SUB] for b in range(batch)]
    for j in range(gp_ref.shape[2] // LANES):
        finish(j, proj, u_ref, k_ref, halo_p, halo_u, inner_ref, gp_ref, j * LANES, gpt)
    if parts:
        hand_out(where_ref[0], gpt, *parts)


def late_kernel(
    col, where_ref, u_ref, k_ref, pair_ref, far_ref, proj, halo_ref,
    gp_ref, mine_ref, send_ref, wide, out, gpt,
):
    batch, rows, feats = u_ref.shape
    chans = pair_ref.shape[1] - feats
    halo_u = halo_of(where_ref, pair_ref, far_ref, chans, pair_ref.shape[1], batch)
    halo_p = [halo_ref[b] for b in range(batch)]
    for t in range(gp_ref.shape[2] // LANES):
        j = col // LANES + t
        inner_gradients(j, proj, u_ref, k_ref, wide, out, gp_ref, t * LANES)
        finish(j, proj, u_ref, k_ref, halo_p, halo_u, gp_ref, gp_ref, t * LANES, gpt)
    hand_out(where_ref[0], gpt, mine_ref, send_ref)


def early(where, x, w, u, k, pair, far, proj, inner, strips, strip):
    batch, rows, _ = x.shape
    ncol = inner.shape[2]
    parts = [shape((strips, strip, batch * rows), BF16)] * 2 if strips else []
    return pl.pallas_call(
        early_kernel,
        out_shape=[shape(inner.shape, BF16), shape((batch, SUB, w.shape[1]), F32)] + parts,
        in_specs=smem() + vmem(8),
        out_specs=vmem(2 + len(parts)),
        scratch_shapes=[pltpu.VMEM((ncol, batch * rows), BF16)],
        compiler_params=params(),
        cost_estimate=pl.CostEstimate(flops=1_000_000_000, bytes_accessed=4_000_000, transcendentals=0),
        name="early",
    )(where, x, w, u, k, pair, far, proj, inner)


def late(where, u, k, pair, far, proj, halo, col, ncol, strips, strip):
    batch, rows, _ = u.shape
    part = shape((strips, strip, batch * rows), BF16)
    return pl.pallas_call(
        functools.partial(late_kernel, col),
        out_shape=[shape((batch, rows, ncol), BF16), part, part],
        in_specs=smem() + vmem(6),
        out_specs=vmem(3),
        scratch_shapes=sample_scratch(batch, rows) + [pltpu.VMEM((ncol, batch * rows), BF16)],
        compiler_params=params(),
        cost_estimate=pl.CostEstimate(flops=4_000_000_000, bytes_accessed=4_000_000, transcendentals=0),
        name="late",
    )(where, u, k, pair, far, proj, halo)


def own_kernel(x_ref, other_ref, mine_a, mine_b, got_a, out_ref):
    batch, rows, chans = x_ref.shape
    flat = x_ref[...].reshape(batch * rows, chans)
    other = other_ref[...].reshape(batch * rows, chans)
    half = mine_a.shape[0]
    for z in range(half):
        out_ref[half + z] = jnp.dot(mine_b[z], flat, preferred_element_type=F32)
    for z in range(half):
        out_ref[z] = (jnp.dot(mine_a[z], flat, preferred_element_type=F32)
                      + jnp.dot(got_a[z], other, preferred_element_type=F32))


def own(x, other, mine_a, mine_b, got_a):
    half, strip, _ = mine_a.shape
    return pl.pallas_call(
        own_kernel,
        out_shape=shape((2 * half, strip, x.shape[2]), F32),
        in_specs=vmem(5),
        out_specs=vmem(1)[0],
        compiler_params=params(),
        cost_estimate=pl.CostEstimate(flops=1_000_000_000, bytes_accessed=4_000_000, transcendentals=0),
        name="own",
    )(x, other, mine_a, mine_b, got_a)


def pack_kernel(where_ref, other_ref, got_b, sums_ref, out_ref, whole):
    core, zed, dee = where_ref[0], where_ref[1], where_ref[2]
    batch, rows, chans = other_ref.shape
    other = other_ref[...].reshape(batch * rows, chans)
    half, strip, _ = got_b.shape
    for z in range(half):
        whole[z] = sums_ref[half + z] + jnp.dot(got_b[z], other, preferred_element_type=F32)
    left = lax.broadcasted_iota(jnp.int32, (strip // 2, LANES), 1) < LANES // 2
    for z in range(2 * half):
        source = sums_ref.at[z] if z < half else whole.at[z - half]
        for b in range(4):
            slot = jnp.where(core == 0, jnp.bitwise_xor(dee, b), jnp.bitwise_xor(zed, z))
            place = jnp.where(core == 0, z, b)
            full = (3 * (b // 2) + 2 * (b % 2)) * LANES
            rest = (3 * (b // 2) + 1) * LANES
            top, bottom = source[0:strip // 2, rest:rest + LANES], source[strip // 2:strip, rest:rest + LANES]
            if b % 2 == 0:
                packed = jnp.where(left, top, pltpu.roll(bottom, LANES // 2, 1))
            else:
                packed = jnp.where(left, pltpu.roll(top, LANES // 2, 1), bottom)
            out_ref[slot, place, 0:strip] = source[0:strip, full:full + LANES].astype(BF16)
            out_ref[slot, place, strip:strip + strip // 2] = packed.astype(BF16)


def pack(where, other, got_b, sums):
    half, strip, _ = got_b.shape
    return pl.pallas_call(
        pack_kernel,
        out_shape=shape((4, 4, strip + strip // 2, LANES), BF16),
        in_specs=smem() + vmem(3),
        out_specs=vmem(1)[0],
        scratch_shapes=[pltpu.VMEM((half, strip, other.shape[2]), F32)],
        compiler_params=params(),
        name="pack",
    )(where, other, got_b, sums)


def fold_kernel(where_ref, own_ref, one_ref, two_ref, three_ref, *outs):
    core, zed, dee = where_ref[0], where_ref[1], where_ref[2]
    mine = jnp.where(core == 0, zed, dee)
    for k, out in enumerate(outs):
        j = jnp.bitwise_xor(mine, k)
        total = own_ref[0, j].astype(F32) + one_ref[j].astype(F32) + two_ref[j].astype(F32) + three_ref[j].astype(F32)
        out[...] = total.astype(out.dtype)


def fold(where, whole, parts):
    block = parts[0].shape[1:]
    return pl.pallas_call(
        fold_kernel,
        out_shape=[shape(block, F32)] + [shape(block, BF16)] * 3,
        in_specs=smem() + vmem(4),
        out_specs=vmem(4),
        compiler_params=params(),
        name="fold",
    )(where, whole, *parts)


def last_kernel(scale, where_ref, own_ref, one_ref, two_ref, three_ref, out_ref):
    odd = where_ref[2] % 2
    total = own_ref[...] + one_ref[...].astype(F32) + two_ref[...].astype(F32) + three_ref[...].astype(F32)
    total = total * scale
    strip = out_ref.shape[0]
    half = LANES // 2
    full, rest = total[:strip], total[strip:]
    rest = jnp.concatenate([rest[:, :half], rest[:, half:]], axis=0)

    @pl.when(odd == 0)
    def _():
        out_ref[:, :LANES] = full
        out_ref[:, LANES:] = rest

    @pl.when(odd == 1)
    def _():
        out_ref[:, :half] = rest
        out_ref[:, half:] = full


def last(where, parts, scale):
    strip = parts[0].shape[0] * 2 // 3
    return pl.pallas_call(
        functools.partial(last_kernel, scale),
        out_shape=shape((strip, LANES + LANES // 2), F32),
        in_specs=smem() + vmem(4),
        out_specs=vmem(1)[0],
        compiler_params=params(),
        name="last",
    )(where, *parts).T


def near_pairs():
    count = lax.axis_size("seq")
    return [(i, i ^ 1) for i in range(count) if i ^ 1 < count]


def far_pairs():
    count = lax.axis_size("seq")
    pairs = [(i, i - 1 if i % 2 == 0 else i + 1) for i in range(count)]
    return [(a, b) for a, b in pairs if 0 <= b < count]


def exchange(array, one, two):
    n_seq, n_dp = lax.axis_size("seq"), lax.axis_size("dp")
    pairs = [(i, i ^ (two if (i // n_dp) % 2 else one)) for i in range(n_seq * n_dp)]
    return lax.ppermute(array, ("seq", "dp"), pairs)


def spread(where, x, w, u, k, pair, far):
    batch = x.shape[0]
    proj, inner = project(x, w, u, k, w.shape[1])
    gp, _ = early(where, x, w, u, k, pair, far, proj, inner, 0, 0)
    input_grad = jnp.einsum("bpf,cf->bpc", gp, w, preferred_element_type=F32).astype(BF16)
    partial = lax.dot_general(x, gp, (((0, 1), (0, 1)), ((), ())), preferred_element_type=F32)
    over_seq = lax.psum_scatter(partial, "seq", scatter_dimension=1, tiled=True)
    total = lax.psum_scatter(over_seq, "dp", scatter_dimension=0, tiled=True)
    return input_grad, total / (batch * lax.axis_size("dp"))


def on_device(skip_input, upstream, proj_weight, depth_kernel):
    batch, rows, chans = skip_input.shape
    feats = upstream.shape[2]
    n_seq, n_dp = lax.axis_size("seq"), lax.axis_size("dp")
    seq, dee = lax.axis_index("seq"), lax.axis_index("dp")
    core, zed = seq % 2, seq // 2
    where = jnp.stack([core, zed, dee, seq]).astype(jnp.int32)
    strip = feats // n_seq
    strips = n_seq // 4
    ncol = feats // 2

    there = functools.partial(pltpu.with_memory_space_constraint, memory_space=pltpu.HBM)
    pair, far = edges(where, there(skip_input), there(upstream))
    x, w, u, k, pair, far = lax.optimization_barrier(
        (skip_input, proj_weight, upstream, depth_kernel, pair, far))
    pair = lax.ppermute(pair, "seq", near_pairs())
    if n_seq != 8 or n_dp != 4 or chans != 4 * (LANES + LANES // 2):
        return spread(where, x, w, u, k, pair, lax.ppermute(far, "seq", far_pairs()))
    here = functools.partial(pltpu.with_memory_space_constraint, memory_space=pltpu.VMEM)
    other = lax.ppermute(skip_input, "seq", near_pairs())
    far = lax.ppermute(far, "seq", far_pairs())
    x, w, u, k = here(x), here(w), here(u), here(k)
    proj, inner = project(x, w, u, k, ncol)
    gp_a, halo, mine_a, send_a = early(where, x, w, u, k, pair, far, proj, inner, strips, strip)
    got_a = lax.ppermute(send_a, "seq", near_pairs())
    gp_b, mine_b, send_b = late(where, u, k, pair, far, proj, halo, ncol, feats - ncol, strips, strip)
    got_b = lax.ppermute(send_b, "seq", near_pairs())
    sums = own(x, other, mine_a, mine_b, got_a)
    whole = pack(where, other, got_b, sums)

    gp = jnp.concatenate([gp_a, gp_b], axis=2)
    input_grad = jnp.einsum("bpf,cf->bpc", gp, proj_weight, preferred_element_type=F32).astype(BF16)
    z_bits = [m * 2 * n_dp for m in (1, 2, 3)]
    got = [exchange(whole[m], m, z) for m, z in zip((1, 2, 3), z_bits)]
    mine, *messages = fold(where, whole, got)
    got = [exchange(message, z, m) for message, m, z in zip(messages, (1, 2, 3), z_bits)]
    return input_grad, last(where, [mine] + got, 1.0 / (batch * n_dp))


def solution(mesh):
    return jax.shard_map(
        on_device,
        mesh=mesh,
        in_specs=(P("dp", "seq", None), P("dp", "seq", None), P(), P()),
        out_specs=(P("dp", "seq", None), P("dp", "seq")),
        check_vma=False,
    )
```

```python
import functools
import math

import jax
import jax.numpy as jnp
from jax import lax
from jax.experimental import pallas as pl
from jax.experimental.pallas import tpu as pltpu
from jax.sharding import PartitionSpec as P

BF16 = jnp.bfloat16
F32 = jnp.float32
C0 = math.sqrt(2.0 / math.pi)
ALPHA = (0.044715 * C0) ** (1.0 / 3.0)
KAPPA = C0 / ALPHA
LANES = 128
SUB = 8
PAD = 8
FIRST = ((0, 0), (3, 2), (1, 1), (2, 3))
VMEM_BYTES = 14 * 1024 * 1024


def position():
    seq = lax.axis_index("seq")
    return lax.rem(seq, 2), lax.div(seq, 2), lax.axis_index("dp")


def vmem(count):
    return [pl.BlockSpec(memory_space=pltpu.VMEM)] * count


def params():
    return pltpu.CompilerParams(vmem_limit_bytes=VMEM_BYTES)


def shape(dims, dtype):
    return pltpu.VMEM(dims, dtype)


def here(array):
    return pltpu.with_memory_space_constraint(array, pltpu.VMEM)


def edges_kernel(x_ref, u_ref, pair_ref, far_ref, x_low, x_high, u_low, u_high, sems):
    batch, rows, chans = x_ref.shape
    copies = []
    for i, (src, low, high) in enumerate(((x_ref, x_low, x_high), (u_ref, u_low, u_high))):
        copies.append(pltpu.make_async_copy(src.at[:, pl.ds(0, 16), :], low, sems.at[2 * i]))
        copies.append(pltpu.make_async_copy(src.at[:, pl.ds(rows - 16, 16), :], high, sems.at[2 * i + 1]))
    for copy in copies:
        copy.start()
    for copy in copies:
        copy.wait()
    even = position()[0] == 0
    for low, high, lo, hi in ((x_low, x_high, 0, chans), (u_low, u_high, chans, pair_ref.shape[1])):
        first = jnp.concatenate([low[b].astype(F32)[:2] for b in range(batch)], axis=0)
        final = jnp.concatenate([high[b].astype(F32)[14:] for b in range(batch)], axis=0)
        pair_ref[:, lo:hi] = jnp.where(even, final, first).astype(BF16)
        far_ref[:, lo:hi] = jnp.where(even, first, final).astype(BF16)


def edges(x, u):
    batch, _, chans = x.shape
    feats = u.shape[2]
    return pl.pallas_call(
        edges_kernel,
        out_shape=[shape((2 * batch, chans + feats), BF16)] * 2,
        in_specs=[pl.BlockSpec(memory_space=pltpu.HBM)] * 2,
        out_specs=vmem(2),
        scratch_shapes=[pltpu.VMEM((batch, 16, chans), BF16)] * 2 + [pltpu.VMEM((batch, 16, feats), BF16)] * 2
        + [pltpu.SemaphoreType.DMA((4,))],
        compiler_params=params(),
        cost_estimate=pl.CostEstimate(flops=0, bytes_accessed=1_000, transcendentals=0),
        name="edges",
    )(x, u)


def relay_kernel(pair_ref, far_ref, pair_out, far_out):
    pair_out[...] = pair_ref[...]
    far_out[...] = far_ref[...]


def relay(pair, far):
    return pl.pallas_call(
        relay_kernel,
        out_shape=[shape(pair.shape, BF16)] * 2,
        in_specs=vmem(2),
        out_specs=vmem(2),
        compiler_params=params(),
        cost_estimate=pl.CostEstimate(flops=10_000_000_000, bytes_accessed=1_000_000, transcendentals=0),
        name="relay",
    )(here(pair), here(far))


def odd_slope(w):
    w2 = w * w
    t = jnp.tanh(w * (w2 + KAPPA))
    return t + w * (w2 + KAPPA / 3.0) * (3.0 - 3.0 * (t * t))


def tap_sets(taps):
    k_sum, k_dif, k_mid = 0.5 * (taps[0:1] + taps[2:3]), 0.5 * (taps[0:1] - taps[2:3]), taps[1:2]
    return (ALPHA * k_sum, ALPHA * k_dif, ALPHA * k_mid), (0.25 * k_sum, 0.25 * k_dif, 0.25 * k_mid)


def slopes(scaled, before, centre, after, u):
    p_sum, p_dif, p_mid = scaled
    same = p_mid * centre + p_sum * (before + after)
    skew = p_dif * (before - after)
    fwd, rev = odd_slope(same + skew), odd_slope(same - skew)
    return u * (2.0 + (fwd + rev)), u * (fwd - rev)


def inner_gradients(j, proj, u_ref, k_ref, wide, out, gp_ref, gp_lane):
    batch, rows = u_ref.shape[:2]
    seg = rows // SUB
    pitch = proj.shape[2] // SUB
    lanes = slice(j * LANES, (j + 1) * LANES)
    scaled, (g_sum, g_dif, g_mid) = tap_sets(k_ref[:, lanes])
    for b in range(batch):
        for s in range(SUB):
            wide[b, s * pitch:s * pitch + seg] = u_ref[b, s * seg:(s + 1) * seg, lanes].astype(F32)
    for b in range(batch):
        def vector(i, b=b):
            return proj[j, b, pl.ds(i, SUB, stride=pitch), :]

        def put(i, before, centre, after, dif_before, dif_after, b=b):
            out[b, pl.ds(i, SUB, stride=pitch), :] = (
                g_mid * centre + g_sum * (before + after) + g_dif * (dif_after - dif_before))

        head, tail = vector(0), vector(seg - 1)
        before, stop = pltpu.roll(tail, 1, 0), pltpu.roll(head, SUB - 1, 0)
        sums, difs = [], []
        centre = head
        for i in range(seg):
            after = stop if i == seg - 1 else (tail if i == seg - 2 else vector(i + 1))
            one, two = slopes(scaled, before, centre, after, wide[b, pl.ds(i, SUB, stride=pitch), :])
            sums.append(one)
            difs.append(two)
            before, centre = centre, after
            if i >= 2:
                put(i - 1, sums[i - 2], sums[i - 1], sums[i], difs[i - 2], difs[i])
        put(0, pltpu.roll(sums[-1], 1, 0), sums[0], sums[1], pltpu.roll(difs[-1], 1, 0), difs[1])
        put(seg - 1, sums[-2], sums[-1], pltpu.roll(sums[0], SUB - 1, 0), difs[-2], pltpu.roll(difs[0], SUB - 1, 0))
        done = jnp.concatenate([out[b, s * pitch:s * pitch + seg] for s in range(SUB)], axis=0)
        gp_ref[b, :, gp_lane:gp_lane + LANES] = done.astype(BF16)


def project_kernel(x_ref, w_ref, u_ref, k_ref, proj, gp_ref, wide, out):
    batch, rows, _ = x_ref.shape
    seg = rows // SUB
    pitch = proj.shape[2] // SUB
    tiles = gp_ref.shape[2] // LANES
    for b in range(batch):
        body = jnp.dot(x_ref[b], w_ref[...], preferred_element_type=F32).astype(BF16).astype(F32)
        for j in range(proj.shape[0]):
            for s in range(SUB):
                proj[j, b, s * pitch:s * pitch + seg] = body[s * seg:(s + 1) * seg, j * LANES:(j + 1) * LANES]
    for j in range(tiles):
        inner_gradients(j, proj, u_ref, k_ref, wide, out, gp_ref, j * LANES)


def sample_scratch(batch, rows):
    return [pltpu.VMEM((batch, rows + SUB * PAD, LANES), F32)] * 2


def project(x, w, u, k, ncol):
    batch, rows, _ = x.shape
    feats = w.shape[1]
    return pl.pallas_call(
        project_kernel,
        out_shape=[shape((feats // LANES, batch, rows + SUB * PAD, LANES), F32), shape((batch, rows, ncol), BF16)],
        in_specs=vmem(4),
        out_specs=vmem(2),
        scratch_shapes=sample_scratch(batch, rows),
        compiler_params=params(),
        cost_estimate=pl.CostEstimate(flops=4_000_000_000, bytes_accessed=4_000_000, transcendentals=0),
        name="project",
    )(*map(here, (x, w, u, k)))


def around(low, high):
    return jnp.concatenate([low, jnp.zeros((SUB - 4, low.shape[1]), low.dtype), high], axis=0)


def halo_of(pair_ref, far_ref, lo, hi, batch):
    even = position()[0] == 0
    pair, far = pair_ref[:, lo:hi].astype(F32), far_ref[:, lo:hi].astype(F32)
    low, high = jnp.where(even, far, pair), jnp.where(even, pair, far)
    return [around(low[2 * b:2 * b + 2], high[2 * b:2 * b + 2]) for b in range(batch)]


def finish(j, proj, u_ref, k_ref, halo_p, halo_u, inner_ref, gp_ref, gp_lane, gpt):
    batch, rows = u_ref.shape[:2]
    pitch = proj.shape[2] // SUB
    seg = rows // SUB
    lanes = slice(j * LANES, (j + 1) * LANES)
    cols = slice(gp_lane, gp_lane + LANES)
    scaled, (g_sum, g_dif, g_mid) = tap_sets(k_ref[:, lanes])
    sub = lax.broadcasted_iota(jnp.int32, (SUB, LANES), 0)

    def centred(low, high, halo):
        ends = jnp.where(sub == 0, pltpu.roll(halo, SUB - 1, 0), pltpu.roll(halo, 1, 0))
        inside = jnp.where(sub < 4, pltpu.roll(low, 1, 0), pltpu.roll(high, SUB - 1, 0))
        return jnp.where(jnp.logical_or(sub == 0, sub == SUB - 1), ends, inside)

    for b in range(batch):
        low = proj[j, b, 0:SUB]
        high = proj[j, b, (SUB - 1) * pitch + seg - SUB:(SUB - 1) * pitch + seg]
        halo = halo_p[b][:, lanes]
        before = jnp.where(sub < 2, halo, jnp.where(sub < 4, pltpu.roll(low, 2, 0), high))
        after = jnp.where(sub < 4, low, jnp.where(sub < 6, pltpu.roll(high, SUB - 2, 0), halo))
        u_low = u_ref[b, 0:16, lanes].astype(F32)[:SUB]
        u_high = u_ref[b, rows - 16:rows, lanes].astype(F32)[16 - SUB:]
        u = centred(u_low, u_high, halo_u[b][:, lanes])
        sums, difs = slopes(scaled, before, centred(low, high, halo), after, u)
        ends = (g_mid * sums + g_sum * (pltpu.roll(sums, 1, 0) + pltpu.roll(sums, SUB - 1, 0))
                + g_dif * (pltpu.roll(difs, SUB - 1, 0) - pltpu.roll(difs, 1, 0)))
        first = inner_ref[b, 0:16, cols].astype(F32)
        last_rows = inner_ref[b, rows - 16:rows, cols].astype(F32)
        first = jnp.concatenate([jnp.where(sub < 2, pltpu.roll(ends, SUB - 1, 0), first[:SUB]), first[SUB:]], axis=0)
        last_rows = jnp.concatenate(
            [last_rows[:SUB], jnp.where(sub >= 6, pltpu.roll(ends, 1, 0), last_rows[SUB:])], axis=0)
        gp_ref[b, 0:16, cols] = first.astype(BF16)
        gp_ref[b, rows - 16:rows, cols] = last_rows.astype(BF16)
        if inner_ref is not gp_ref:
            gp_ref[b, 16:rows - 16, cols] = inner_ref[b, 16:rows - 16, cols]
        gpt[cols, b * rows:(b + 1) * rows] = gp_ref[b, :, cols].T


def hand_out(core, gpt, mine_ref, send_ref):
    strip = mine_ref.shape[1]
    for z in range(mine_ref.shape[0]):
        for result, who in ((mine_ref, core), (send_ref, 1 - core)):
            result[z] = gpt[pl.ds(pl.multiple_of((2 * z + who) * strip, 16), strip), :]


def early_kernel(
    x_ref, w_ref, u_ref, k_ref, pair_ref, far_ref, proj, inner_ref,
    gp_ref, halo_ref, *rest,
):
    *parts, gpt = rest
    batch, rows, chans = x_ref.shape
    halo_x = halo_of(pair_ref, far_ref, 0, chans, batch)
    halo_u = halo_of(pair_ref, far_ref, chans, pair_ref.shape[1], batch)
    halo_x = jnp.concatenate(halo_x, axis=0).astype(BF16)
    halo_all = jnp.dot(halo_x, w_ref[...], preferred_element_type=F32).astype(BF16).astype(F32)
    for b in range(batch):
        halo_ref[b] = halo_all[b * SUB:(b + 1) * SUB]
    halo_p = [halo_all[b * SUB:(b + 1) * SUB] for b in range(batch)]
    for j in range(gp_ref.shape[2] // LANES):
        finish(j, proj, u_ref, k_ref, halo_p, halo_u, inner_ref, gp_ref, j * LANES, gpt)
    if parts:
        hand_out(position()[0], gpt, *parts)


def late_kernel(
    col, u_ref, k_ref, pair_ref, far_ref, proj, halo_ref,
    gp_ref, mine_ref, send_ref, wide, out, gpt,
):
    batch, rows, feats = u_ref.shape
    chans = pair_ref.shape[1] - feats
    halo_u = halo_of(pair_ref, far_ref, chans, pair_ref.shape[1], batch)
    halo_p = [halo_ref[b] for b in range(batch)]
    for t in range(gp_ref.shape[2] // LANES):
        j = col // LANES + t
        inner_gradients(j, proj, u_ref, k_ref, wide, out, gp_ref, t * LANES)
        finish(j, proj, u_ref, k_ref, halo_p, halo_u, gp_ref, gp_ref, t * LANES, gpt)
    hand_out(position()[0], gpt, mine_ref, send_ref)


def early(x, w, u, k, pair, far, proj, inner, strips, strip):
    batch, rows, _ = x.shape
    ncol = inner.shape[2]
    parts = [shape((strips, strip, batch * rows), BF16)] * 2 if strips else []
    return pl.pallas_call(
        early_kernel,
        out_shape=[shape(inner.shape, BF16), shape((batch, SUB, w.shape[1]), F32)] + parts,
        in_specs=vmem(8),
        out_specs=vmem(2 + len(parts)),
        scratch_shapes=[pltpu.VMEM((ncol, batch * rows), BF16)],
        compiler_params=params(),
        cost_estimate=pl.CostEstimate(flops=1_000_000_000, bytes_accessed=4_000_000, transcendentals=0),
        name="early",
    )(*map(here, (x, w, u, k, pair, far, proj, inner)))


def late(u, k, pair, far, proj, halo, col, ncol, strips, strip):
    batch, rows, _ = u.shape
    part = shape((strips, strip, batch * rows), BF16)
    return pl.pallas_call(
        functools.partial(late_kernel, col),
        out_shape=[shape((batch, rows, ncol), BF16), part, part],
        in_specs=vmem(6),
        out_specs=vmem(3),
        scratch_shapes=sample_scratch(batch, rows) + [pltpu.VMEM((ncol, batch * rows), BF16)],
        compiler_params=params(),
        cost_estimate=pl.CostEstimate(flops=4_000_000_000, bytes_accessed=4_000_000, transcendentals=0),
        name="late",
    )(*map(here, (u, k, pair, far, proj, halo)))


def own_kernel(x_ref, other_ref, mine_a, mine_b, got_a, out_ref):
    batch, rows, chans = x_ref.shape
    flat = x_ref[...].reshape(batch * rows, chans)
    other = other_ref[...].reshape(batch * rows, chans)
    half = mine_a.shape[0]
    for z in range(half):
        out_ref[half + z] = jnp.dot(mine_b[z], flat, preferred_element_type=F32)
    for z in range(half):
        out_ref[z] = (jnp.dot(mine_a[z], flat, preferred_element_type=F32)
                      + jnp.dot(got_a[z], other, preferred_element_type=F32))


def own(x, other, mine_a, mine_b, got_a):
    half, strip, _ = mine_a.shape
    return pl.pallas_call(
        own_kernel,
        out_shape=shape((2 * half, strip, x.shape[2]), F32),
        in_specs=vmem(5),
        out_specs=vmem(1)[0],
        compiler_params=params(),
        cost_estimate=pl.CostEstimate(flops=1_000_000_000, bytes_accessed=4_000_000, transcendentals=0),
        name="own",
    )(*map(here, (x, other, mine_a, mine_b, got_a)))


def pack_kernel(other_ref, got_b, sums_in, sums_ref, *outs):
    core, zed, dee = position()
    batch, rows, chans = other_ref.shape
    other = other_ref[...].reshape(batch * rows, chans)
    half, strip, _ = got_b.shape
    for z in range(half):
        sums_ref[half + z] = sums_in[half + z] + jnp.dot(got_b[z], other, preferred_element_type=F32)
    left = lax.broadcasted_iota(jnp.int32, (strip // 2, LANES), 1) < LANES // 2
    for (d_turn, z_turn), out in zip(FIRST, outs):
        for j in range(4):
            z = jnp.where(core == 0, j, jnp.bitwise_xor(zed, z_turn))
            b = jnp.where(core == 0, jnp.bitwise_xor(dee, d_turn), j)
            y, odd = lax.div(b, 2), lax.rem(b, 2)
            full = pl.multiple_of((3 * y + 2 * odd) * LANES, LANES)
            rest = pl.multiple_of((3 * y + 1) * LANES, LANES)
            top, bottom = sums_ref[z, 0:strip // 2, pl.ds(rest, LANES)], sums_ref[z, strip // 2:strip, pl.ds(rest, LANES)]
            turned = pltpu.roll(jnp.where(left, bottom, top), LANES // 2, 1)
            kept = jnp.where(odd == 0, top, bottom)
            out[j, 0:strip] = sums_ref[z, :, pl.ds(full, LANES)].astype(out.dtype)
            out[j, strip:strip + strip // 2] = jnp.where(left == (odd == 0), kept, turned).astype(out.dtype)


def pack(other, got_b, sums):
    half, strip, _ = got_b.shape
    block = (4, strip + strip // 2, LANES)
    return pl.pallas_call(
        pack_kernel,
        out_shape=[shape(sums.shape, F32), shape(block, F32)] + [shape(block, BF16)] * 3,
        in_specs=vmem(3),
        out_specs=vmem(5),
        input_output_aliases={2: 0},
        compiler_params=params(),
        name="pack",
    )(*map(here, (other, got_b, sums)))[1:]


def fold_kernel(own_ref, one_ref, two_ref, three_ref, token, *outs):
    core, zed, dee = position()
    mine = jnp.where(core == 0, zed, dee)
    for k in (3, 2, 1, 0):
        j = jnp.bitwise_xor(mine, k)
        total = own_ref[j] + one_ref[j].astype(F32) + two_ref[j].astype(F32) + three_ref[j].astype(F32)
        outs[k][...] = total.astype(outs[k].dtype)


def fold(parts, token):
    block = parts[0].shape[1:]
    return pl.pallas_call(
        fold_kernel,
        out_shape=[shape(block, F32)] + [shape(block, BF16)] * 3,
        in_specs=vmem(5),
        out_specs=vmem(4),
        compiler_params=params(),
        name="fold",
    )(*map(here, parts), here(token))


def input_kernel(gp_a, gp_b, w_ref, out_ref, token):
    token[...] = jnp.zeros_like(token)
    cut = gp_a.shape[2]
    for b in range(out_ref.shape[0]):
        total = lax.dot_general(gp_a[b], w_ref[:, :cut], (((1,), (1,)), ((), ())), preferred_element_type=F32)
        total += lax.dot_general(gp_b[b], w_ref[:, cut:], (((1,), (1,)), ((), ())), preferred_element_type=F32)
        out_ref[b] = total.astype(BF16)


def input_gradient(gp_a, gp_b, w):
    batch, rows, _ = gp_a.shape
    return pl.pallas_call(
        input_kernel,
        out_shape=[jax.ShapeDtypeStruct((batch, rows, w.shape[0]), BF16), shape((SUB, LANES), F32)],
        in_specs=vmem(3),
        out_specs=vmem(2),
        compiler_params=params(),
        cost_estimate=pl.CostEstimate(flops=2_000_000_000, bytes_accessed=1_000_000, transcendentals=0),
        name="input_gradient",
    )(here(gp_a), here(gp_b), here(w))


def last_kernel(scale, own_ref, one_ref, two_ref, three_ref, out_ref):
    odd = lax.rem(position()[2], 2)
    total = own_ref[...] + one_ref[...].astype(F32) + two_ref[...].astype(F32) + three_ref[...].astype(F32)
    total = total * scale
    strip = out_ref.shape[0]
    half = LANES // 2
    full, rest = total[:strip], total[strip:]
    rest = jnp.concatenate([rest[:, :half], rest[:, half:]], axis=0)

    @pl.when(odd == 0)
    def _():
        out_ref[:, :LANES] = full
        out_ref[:, LANES:] = rest

    @pl.when(odd == 1)
    def _():
        out_ref[:, :half] = rest
        out_ref[:, half:] = full


def last(parts, scale):
    strip = parts[0].shape[0] * 2 // 3
    return pl.pallas_call(
        functools.partial(last_kernel, scale),
        out_shape=jax.ShapeDtypeStruct((strip, LANES + LANES // 2), F32),
        in_specs=vmem(4),
        out_specs=vmem(1)[0],
        compiler_params=params(),
        name="last",
    )(*parts).T


def near_pairs():
    count = lax.axis_size("seq")
    return [(i, i ^ 1) for i in range(count) if i ^ 1 < count]


def far_pairs():
    count = lax.axis_size("seq")
    pairs = [(i, i - 1 if i % 2 == 0 else i + 1) for i in range(count)]
    return [(a, b) for a, b in pairs if 0 <= b < count]


def exchange(array, one, two):
    n_seq, n_dp = lax.axis_size("seq"), lax.axis_size("dp")
    pairs = [(i, i ^ (two if (i // n_dp) % 2 else one)) for i in range(n_seq * n_dp)]
    return lax.ppermute(array, ("seq", "dp"), pairs)


def spread(x, w, u, k, pair, far):
    batch = x.shape[0]
    proj, inner = project(x, w, u, k, w.shape[1])
    gp, _ = early(x, w, u, k, pair, far, proj, inner, 0, 0)
    input_grad = jnp.einsum("bpf,cf->bpc", gp, w, preferred_element_type=F32).astype(BF16)
    partial = lax.dot_general(x, gp, (((0, 1), (0, 1)), ((), ())), preferred_element_type=F32)
    over_seq = lax.psum_scatter(partial, "seq", scatter_dimension=1, tiled=True)
    total = lax.psum_scatter(over_seq, "dp", scatter_dimension=0, tiled=True)
    return input_grad, total / (batch * lax.axis_size("dp"))


def on_device(skip_input, upstream, proj_weight, depth_kernel):
    batch, rows, chans = skip_input.shape
    feats = upstream.shape[2]
    n_seq, n_dp = lax.axis_size("seq"), lax.axis_size("dp")
    seq, dee = lax.axis_index("seq"), lax.axis_index("dp")
    core, zed = seq % 2, seq // 2
    strip = feats // n_seq
    strips = n_seq // 4
    ncol = feats // 2

    there = functools.partial(pltpu.with_memory_space_constraint, memory_space=pltpu.HBM)
    pair, far = edges(there(skip_input), there(upstream))
    pair, far = relay(pair, far)
    x, w, u, k = skip_input, proj_weight, upstream, depth_kernel
    pair = lax.ppermute(pair, "seq", near_pairs())
    if n_seq != 8 or n_dp != 4 or chans != 4 * (LANES + LANES // 2):
        return spread(x, w, u, k, pair, lax.ppermute(far, "seq", far_pairs()))
    other = lax.ppermute(skip_input, "seq", near_pairs())
    far = lax.ppermute(far, "seq", far_pairs())
    proj, inner = project(x, w, u, k, ncol)
    gp_a, halo, mine_a, send_a = early(x, w, u, k, pair, far, proj, inner, strips, strip)
    got_a = lax.ppermute(send_a, "seq", near_pairs())
    gp_b, mine_b, send_b = late(u, k, pair, far, proj, halo, ncol, feats - ncol, strips, strip)
    got_b = lax.ppermute(send_b, "seq", near_pairs())
    sums = own(x, other, mine_a, mine_b, got_a)
    own_blocks, *messages = pack(other, got_b, sums)

    input_grad, token = input_gradient(gp_a, gp_b, w)
    z_bits = [m * 2 * n_dp for m in range(4)]
    got = [exchange(message, d, z_bits[z]) for message, (d, z) in zip(messages, FIRST[1:])]
    own_block, *messages = fold([own_blocks] + got, token)
    got = [exchange(messages[k - 1], z_bits[k], k) for k in (3, 2, 1)]
    return input_grad, last([own_block] + got, 1.0 / (batch * n_dp))


def solution(mesh):
    return jax.shard_map(
        on_device,
        mesh=mesh,
        in_specs=(P("dp", "seq", None), P("dp", "seq", None), P(), P()),
        out_specs=(P("dp", "seq", None), P("dp", "seq")),
        check_vma=False,
    )
```

```python
import functools
import math

import jax
import jax.numpy as jnp
from jax import lax
from jax.experimental import pallas as pl
from jax.experimental.pallas import tpu as pltpu
from jax.sharding import PartitionSpec as P

BF16 = jnp.bfloat16
F32 = jnp.float32
C0 = math.sqrt(2.0 / math.pi)
ALPHA = (0.044715 * C0) ** (1.0 / 3.0)
KAPPA = C0 / ALPHA
LANES = 128
SUB = 8
PAD = 8
HOP = 9
FIRST = ((0, 0), (3, 2), (1, 1), (2, 3))
VMEM_BYTES = 14 * 1024 * 1024


def position():
    seq = lax.axis_index("seq")
    return lax.rem(seq, 2), lax.div(seq, 2), lax.axis_index("dp")


def vmem(count):
    return [pl.BlockSpec(memory_space=pltpu.VMEM)] * count


def params():
    return pltpu.CompilerParams(vmem_limit_bytes=VMEM_BYTES)


def shape(dims, dtype):
    return pltpu.VMEM(dims, dtype)


def here(array):
    return pltpu.with_memory_space_constraint(array, pltpu.VMEM)


def edges_kernel(x_ref, u_ref, far_ref, x_rows, u_rows, sems):
    batch, rows, chans = x_ref.shape
    even = position()[0] == 0
    start = pl.multiple_of(jnp.where(even, 0, rows - 16), 16)
    copies = [
        pltpu.make_async_copy(src.at[:, pl.ds(start, 16), :], dst, sems.at[i])
        for i, (src, dst) in enumerate(((x_ref, x_rows), (u_ref, u_rows)))
    ]
    for copy in copies:
        copy.start()
    for copy in copies:
        copy.wait()
    for held, lo, hi in ((x_rows, 0, chans), (u_rows, chans, far_ref.shape[1])):
        wide = [held[b].astype(F32) for b in range(batch)]
        wide = jnp.concatenate([jnp.where(even, one[:2], one[14:]) for one in wide], axis=0)
        far_ref[:, lo:hi] = wide.astype(BF16)


def edges(x, u):
    batch, _, chans = x.shape
    feats = u.shape[2]
    return pl.pallas_call(
        edges_kernel,
        out_shape=shape((2 * batch, chans + feats), BF16),
        in_specs=[pl.BlockSpec(memory_space=pltpu.HBM)] * 2,
        out_specs=vmem(1)[0],
        scratch_shapes=[pltpu.VMEM((batch, 16, chans), BF16), pltpu.VMEM((batch, 16, feats), BF16),
                        pltpu.SemaphoreType.DMA((2,))],
        compiler_params=params(),
        cost_estimate=pl.CostEstimate(flops=0, bytes_accessed=1_000, transcendentals=0),
        name="edges",
    )(x, u)


def relay_kernel(far_ref, far_out):
    far_out[...] = far_ref[...]


def relay(far):
    return pl.pallas_call(
        relay_kernel,
        out_shape=shape(far.shape, BF16),
        in_specs=vmem(1),
        out_specs=vmem(1)[0],
        compiler_params=params(),
        cost_estimate=pl.CostEstimate(flops=10_000_000_000, bytes_accessed=1_000_000, transcendentals=0),
        name="relay",
    )(here(far))


def slope(w):
    w2 = w * w
    t = jnp.tanh(w * (w2 + KAPPA))
    return (1.0 + t) * (w * (w2 + KAPPA / 3.0) * (1.0 - t) + 1.0 / 3.0)


def tap_sets(taps):
    k_sum, k_dif, k_mid = 0.5 * (taps[0:1] + taps[2:3]), 0.5 * (taps[0:1] - taps[2:3]), taps[1:2]
    return (ALPHA * taps[0:1], ALPHA * taps[1:2], ALPHA * taps[2:3]), (0.75 * k_sum, 0.75 * k_dif, 0.75 * k_mid)


def products(scaled, value):
    return [tap * value for tap in scaled]


def slopes(before, centre, after, u):
    fwd = slope(centre[1] + before[0] + after[2])
    rev = slope(centre[1] + before[2] + after[0])
    return u * (fwd + rev), u * (fwd - rev)


def inner_gradients(j, proj, u_ref, k_ref, wide, out, gp_ref, gp_lane):
    batch, rows = u_ref.shape[:2]
    seg = rows // SUB
    pitch = proj.shape[2] // SUB
    lanes = slice(j * LANES, (j + 1) * LANES)
    scaled, (g_sum, g_dif, g_mid) = tap_sets(k_ref[:, lanes])
    for b in range(batch):
        for s in range(SUB):
            wide[b, s * pitch:s * pitch + seg] = u_ref[b, s * seg:(s + 1) * seg, lanes].astype(F32)
    for b in range(batch):
        def vector(i, b=b):
            return products(scaled, proj[j, b, pl.ds(i, SUB, stride=pitch), :])

        def put(i, before, centre, after, dif_before, dif_after, b=b):
            out[b, i * HOP:i * HOP + SUB, :] = (
                g_mid * centre + g_sum * (before + after) + g_dif * (dif_after - dif_before))

        head, tail = vector(0), vector(seg - 1)
        before, stop = [pltpu.roll(one, 1, 0) for one in tail], [pltpu.roll(one, SUB - 1, 0) for one in head]
        sums, difs = [], []
        centre = head
        for i in range(seg):
            after = stop if i == seg - 1 else (tail if i == seg - 2 else vector(i + 1))
            one, two = slopes(before, centre, after, wide[b, pl.ds(i, SUB, stride=pitch), :])
            sums.append(one)
            difs.append(two)
            before, centre = centre, after
            if i >= 2:
                put(i - 1, sums[i - 2], sums[i - 1], sums[i], difs[i - 2], difs[i])
        put(0, pltpu.roll(sums[-1], 1, 0), sums[0], sums[1], pltpu.roll(difs[-1], 1, 0), difs[1])
        put(seg - 1, sums[-2], sums[-1], pltpu.roll(sums[0], SUB - 1, 0), difs[-2], pltpu.roll(difs[0], SUB - 1, 0))
        done = jnp.concatenate(
            [out[b, pl.ds(lo * HOP + s, SUB, stride=HOP), :] for s in range(SUB) for lo in range(0, seg, SUB)], axis=0)
        gp_ref[b, :, gp_lane:gp_lane + LANES] = done.astype(BF16)


def project_kernel(x_ref, w_ref, u_ref, k_ref, proj, gp_ref, wide, out):
    batch, rows, _ = x_ref.shape
    seg = rows // SUB
    pitch = proj.shape[2] // SUB
    tiles = gp_ref.shape[2] // LANES
    for b in range(batch):
        body = jnp.dot(x_ref[b], w_ref[...], preferred_element_type=F32).astype(BF16).astype(F32)
        for j in range(proj.shape[0]):
            for s in range(SUB):
                proj[j, b, s * pitch:s * pitch + seg] = body[s * seg:(s + 1) * seg, j * LANES:(j + 1) * LANES]
    for j in range(tiles):
        inner_gradients(j, proj, u_ref, k_ref, wide, out, gp_ref, j * LANES)


def sample_scratch(batch, rows):
    return [pltpu.VMEM((batch, rows + SUB * PAD, LANES), F32), pltpu.VMEM((batch, rows // SUB * HOP, LANES), F32)]


def project(x, w, u, k, ncol):
    batch, rows, _ = x.shape
    feats = w.shape[1]
    return pl.pallas_call(
        project_kernel,
        out_shape=[shape((feats // LANES, batch, rows + SUB * PAD, LANES), F32), shape((batch, rows, ncol), BF16)],
        in_specs=vmem(4),
        out_specs=vmem(2),
        scratch_shapes=sample_scratch(batch, rows),
        compiler_params=params(),
        cost_estimate=pl.CostEstimate(flops=4_000_000_000, bytes_accessed=4_000_000, transcendentals=0),
        name="project",
    )(*map(here, (x, w, u, k)))


def around(low, high):
    return jnp.concatenate([low, jnp.zeros((SUB - 4, low.shape[1]), low.dtype), high], axis=0)


def halo_of(pair_ref, far_rows):
    batch, rows, _ = pair_ref.shape
    even = position()[0] == 0
    far_rows = far_rows.astype(F32)
    result = []
    for b in range(batch):
        far = far_rows[2 * b:2 * b + 2]
        low, high = pair_ref[b, rows - 16:rows].astype(F32)[14:], pair_ref[b, 0:16].astype(F32)[:2]
        result.append(around(jnp.where(even, far, low), jnp.where(even, high, far)))
    return result


def finish(j, proj, u_ref, k_ref, halo_p, halo_u, inner_ref, gp_ref, gp_lane, gpt):
    batch, rows = u_ref.shape[:2]
    pitch = proj.shape[2] // SUB
    seg = rows // SUB
    lanes = slice(j * LANES, (j + 1) * LANES)
    cols = slice(gp_lane, gp_lane + LANES)
    scaled, (g_sum, g_dif, g_mid) = tap_sets(k_ref[:, lanes])
    sub = lax.broadcasted_iota(jnp.int32, (SUB, LANES), 0)

    def centred(low, high, halo):
        ends = jnp.where(sub == 0, pltpu.roll(halo, SUB - 1, 0), pltpu.roll(halo, 1, 0))
        inside = jnp.where(sub < 4, pltpu.roll(low, 1, 0), pltpu.roll(high, SUB - 1, 0))
        return jnp.where(jnp.logical_or(sub == 0, sub == SUB - 1), ends, inside)

    for b in range(batch):
        low = proj[j, b, 0:SUB]
        high = proj[j, b, (SUB - 1) * pitch + seg - SUB:(SUB - 1) * pitch + seg]
        halo = halo_p[b][:, lanes]
        before = jnp.where(sub < 2, halo, jnp.where(sub < 4, pltpu.roll(low, 2, 0), high))
        after = jnp.where(sub < 4, low, jnp.where(sub < 6, pltpu.roll(high, SUB - 2, 0), halo))
        u_low = u_ref[b, 0:16, lanes].astype(F32)[:SUB]
        u_high = u_ref[b, rows - 16:rows, lanes].astype(F32)[16 - SUB:]
        u = centred(u_low, u_high, halo_u[b][:, lanes])
        sums, difs = slopes(*(products(scaled, one) for one in (before, centred(low, high, halo), after)), u)
        ends = (g_mid * sums + g_sum * (pltpu.roll(sums, 1, 0) + pltpu.roll(sums, SUB - 1, 0))
                + g_dif * (pltpu.roll(difs, SUB - 1, 0) - pltpu.roll(difs, 1, 0)))
        first = inner_ref[b, 0:16, cols].astype(F32)
        last_rows = inner_ref[b, rows - 16:rows, cols].astype(F32)
        first = jnp.concatenate([jnp.where(sub < 2, pltpu.roll(ends, SUB - 1, 0), first[:SUB]), first[SUB:]], axis=0)
        last_rows = jnp.concatenate(
            [last_rows[:SUB], jnp.where(sub >= 6, pltpu.roll(ends, 1, 0), last_rows[SUB:])], axis=0)
        gp_ref[b, 0:16, cols] = first.astype(BF16)
        gp_ref[b, rows - 16:rows, cols] = last_rows.astype(BF16)
        if inner_ref is not gp_ref:
            gp_ref[b, 16:rows - 16, cols] = inner_ref[b, 16:rows - 16, cols]
        gpt[cols, b * rows:(b + 1) * rows] = gp_ref[b, :, cols].T


def hand_out(core, gpt, mine_ref, send_ref):
    strip = mine_ref.shape[1]
    for z in range(mine_ref.shape[0]):
        for result, who in ((mine_ref, core), (send_ref, 1 - core)):
            result[z] = gpt[pl.ds(pl.multiple_of((2 * z + who) * strip, 16), strip), :]


def early_kernel(
    x_ref, w_ref, u_ref, k_ref, pair_x, pair_u, far_ref, proj, inner_ref,
    gp_ref, halo_ref, halo_u_ref, *rest,
):
    *parts, gpt = rest
    batch, rows, chans = x_ref.shape
    halo_x = halo_of(pair_x, far_ref[:, :chans])
    halo_u = halo_of(pair_u, far_ref[:, chans:])
    for b in range(batch):
        halo_u_ref[b] = halo_u[b]
    halo_x = jnp.concatenate(halo_x, axis=0).astype(BF16)
    halo_all = jnp.dot(halo_x, w_ref[...], preferred_element_type=F32).astype(BF16).astype(F32)
    for b in range(batch):
        halo_ref[b] = halo_all[b * SUB:(b + 1) * SUB]
    halo_p = [halo_all[b * SUB:(b + 1) * SUB] for b in range(batch)]
    for j in range(gp_ref.shape[2] // LANES):
        finish(j, proj, u_ref, k_ref, halo_p, halo_u, inner_ref, gp_ref, j * LANES, gpt)
    if parts:
        hand_out(position()[0], gpt, *parts)


def late_kernel(
    col, u_ref, k_ref, proj, halo_ref, halo_u_ref,
    gp_ref, mine_ref, send_ref, wide, out, gpt,
):
    batch, rows, feats = u_ref.shape
    halo_u = [halo_u_ref[b] for b in range(batch)]
    halo_p = [halo_ref[b] for b in range(batch)]
    for t in range(gp_ref.shape[2] // LANES):
        j = col // LANES + t
        inner_gradients(j, proj, u_ref, k_ref, wide, out, gp_ref, t * LANES)
        finish(j, proj, u_ref, k_ref, halo_p, halo_u, gp_ref, gp_ref, t * LANES, gpt)
    hand_out(position()[0], gpt, mine_ref, send_ref)


def early(x, w, u, k, pair_x, pair_u, far, proj, inner, strips, strip):
    batch, rows, _ = x.shape
    ncol = inner.shape[2]
    parts = [shape((strips, strip, batch * rows), BF16)] * 2 if strips else []
    return pl.pallas_call(
        early_kernel,
        out_shape=[shape(inner.shape, BF16)] + [shape((batch, SUB, w.shape[1]), F32)] * 2 + parts,
        in_specs=vmem(9),
        out_specs=vmem(3 + len(parts)),
        scratch_shapes=[pltpu.VMEM((ncol, batch * rows), BF16)],
        compiler_params=params(),
        cost_estimate=pl.CostEstimate(flops=1_000_000_000, bytes_accessed=4_000_000, transcendentals=0),
        name="early",
    )(*map(here, (x, w, u, k, pair_x, pair_u, far, proj, inner)))


def late(u, k, proj, halo, halo_u, col, ncol, strips, strip):
    batch, rows, _ = u.shape
    part = shape((strips, strip, batch * rows), BF16)
    return pl.pallas_call(
        functools.partial(late_kernel, col),
        out_shape=[shape((batch, rows, ncol), BF16), part, part],
        in_specs=vmem(5),
        out_specs=vmem(3),
        scratch_shapes=sample_scratch(batch, rows) + [pltpu.VMEM((ncol, batch * rows), BF16)],
        compiler_params=params(),
        cost_estimate=pl.CostEstimate(flops=4_000_000_000, bytes_accessed=4_000_000, transcendentals=0),
        name="late",
    )(*map(here, (u, k, proj, halo, halo_u)))


def stacked(ref):
    return ref[...].reshape(ref.shape[0] * ref.shape[1], ref.shape[2])


def place_blocks(strips, sums_ref, out_ref):
    core, zed, dee = position()
    strip = sums_ref.shape[1]
    half = strip // 2
    left = lax.broadcasted_iota(jnp.int32, (half, LANES), 1) < LANES // 2

    def slot(turn, turns):
        return sum(jnp.where(turn == one, at, 0) for at, one in enumerate(turns))

    for z in strips:
        z_slot = slot(jnp.bitwise_xor(zed, z), [pair[1] for pair in FIRST])
        for b in range(4):
            b_slot = slot(jnp.bitwise_xor(dee, b), [pair[0] for pair in FIRST])
            at, spot = jnp.where(core == 0, b_slot, z_slot), jnp.where(core == 0, z, b)
            full = (3 * (b // 2) + 2 * (b % 2)) * LANES
            rest = (3 * (b // 2) + 1) * LANES
            top, bottom = sums_ref[z, 0:half, rest:rest + LANES], sums_ref[z, half:strip, rest:rest + LANES]
            if b % 2 == 0:
                packed = jnp.where(left, top, pltpu.roll(bottom, LANES // 2, 1))
            else:
                packed = jnp.where(left, pltpu.roll(top, LANES // 2, 1), bottom)
            out_ref[at, spot, 0:strip] = sums_ref[z, :, full:full + LANES].astype(BF16)
            out_ref[at, spot, strip:strip + half] = packed.astype(BF16)


def own_kernel(x_ref, other_ref, mine_a, mine_b, got_a, sums_ref, out_ref):
    flat, other = stacked(x_ref), stacked(other_ref)
    half, strip, _ = mine_a.shape
    later = jnp.dot(stacked(mine_b), flat, preferred_element_type=F32)
    sooner = (jnp.dot(stacked(mine_a), flat, preferred_element_type=F32)
              + jnp.dot(stacked(got_a), other, preferred_element_type=F32))
    for z in range(half):
        sums_ref[half + z] = later[z * strip:(z + 1) * strip]
        sums_ref[z] = sooner[z * strip:(z + 1) * strip]
    place_blocks(range(half), sums_ref, out_ref)


def own(x, other, mine_a, mine_b, got_a):
    half, strip, _ = mine_a.shape
    return pl.pallas_call(
        own_kernel,
        out_shape=[shape((2 * half, strip, x.shape[2]), F32), shape((4, 4, strip + strip // 2, LANES), BF16)],
        in_specs=vmem(5),
        out_specs=vmem(2),
        compiler_params=params(),
        cost_estimate=pl.CostEstimate(flops=1_000_000_000, bytes_accessed=4_000_000, transcendentals=0),
        name="own",
    )(*map(here, (x, other, mine_a, mine_b, got_a)))


def pack_kernel(other_ref, got_b, sums_in, blocks_in, sums_ref, out_ref):
    half, strip, _ = got_b.shape
    later = jnp.dot(stacked(got_b), stacked(other_ref), preferred_element_type=F32)
    for z in range(half):
        sums_ref[half + z] = sums_in[half + z] + later[z * strip:(z + 1) * strip]
    place_blocks(range(half, 2 * half), sums_ref, out_ref)


def pack(other, got_b, sums, blocks):
    return pl.pallas_call(
        pack_kernel,
        out_shape=[shape(sums.shape, F32), shape(blocks.shape, BF16)],
        in_specs=vmem(4),
        out_specs=vmem(2),
        input_output_aliases={2: 0, 3: 1},
        compiler_params=params(),
        name="pack",
    )(*map(here, (other, got_b, sums, blocks)))[1]


def fold_kernel(own_ref, one_ref, two_ref, three_ref, token, *outs):
    core, zed, dee = position()
    mine = jnp.where(core == 0, zed, dee)
    for k in (3, 2, 1, 0):
        j = jnp.bitwise_xor(mine, k)
        total = own_ref[0, j].astype(F32) + one_ref[j].astype(F32) + two_ref[j].astype(F32) + three_ref[j].astype(F32)
        outs[k][...] = total.astype(outs[k].dtype)


def fold(parts, token):
    block = parts[1].shape[1:]
    return pl.pallas_call(
        fold_kernel,
        out_shape=[shape(block, F32)] + [shape(block, BF16)] * 3,
        in_specs=vmem(5),
        out_specs=vmem(4),
        compiler_params=params(),
        name="fold",
    )(*map(here, parts), here(token))


def input_kernel(gp_a, gp_b, w_ref, out_ref, token):
    token[...] = jnp.zeros_like(token)
    cut = gp_a.shape[2]
    for b in range(out_ref.shape[0]):
        total = lax.dot_general(gp_a[b], w_ref[:, :cut], (((1,), (1,)), ((), ())), preferred_element_type=F32)
        total += lax.dot_general(gp_b[b], w_ref[:, cut:], (((1,), (1,)), ((), ())), preferred_element_type=F32)
        out_ref[b] = total.astype(BF16)


def input_gradient(gp_a, gp_b, w):
    batch, rows, _ = gp_a.shape
    return pl.pallas_call(
        input_kernel,
        out_shape=[jax.ShapeDtypeStruct((batch, rows, w.shape[0]), BF16), shape((SUB, LANES), F32)],
        in_specs=vmem(3),
        out_specs=vmem(2),
        compiler_params=params(),
        cost_estimate=pl.CostEstimate(flops=2_000_000_000, bytes_accessed=1_000_000, transcendentals=0),
        name="input_gradient",
    )(here(gp_a), here(gp_b), here(w))


def last_kernel(scale, own_ref, one_ref, two_ref, three_ref, out_ref):
    odd = lax.rem(position()[2], 2)
    total = own_ref[...] + one_ref[...].astype(F32) + two_ref[...].astype(F32) + three_ref[...].astype(F32)
    total = total * scale
    strip = out_ref.shape[0]
    half = LANES // 2
    full, rest = total[:strip], total[strip:]
    rest = jnp.concatenate([rest[:, :half], rest[:, half:]], axis=0)

    @pl.when(odd == 0)
    def _():
        out_ref[:, :LANES] = full
        out_ref[:, LANES:] = rest

    @pl.when(odd == 1)
    def _():
        out_ref[:, :half] = rest
        out_ref[:, half:] = full


def last(parts, scale):
    strip = parts[0].shape[0] * 2 // 3
    return pl.pallas_call(
        functools.partial(last_kernel, scale),
        out_shape=jax.ShapeDtypeStruct((strip, LANES + LANES // 2), F32),
        in_specs=vmem(4),
        out_specs=vmem(1)[0],
        compiler_params=params(),
        name="last",
    )(*parts).T


def near_pairs():
    count = lax.axis_size("seq")
    return [(i, i ^ 1) for i in range(count) if i ^ 1 < count]


def far_pairs():
    count = lax.axis_size("seq")
    pairs = [(i, i - 1 if i % 2 == 0 else i + 1) for i in range(count)]
    return [(a, b) for a, b in pairs if 0 <= b < count]


def exchange(array, one, two):
    n_seq, n_dp = lax.axis_size("seq"), lax.axis_size("dp")
    pairs = [(i, i ^ (two if (i // n_dp) % 2 else one)) for i in range(n_seq * n_dp)]
    return lax.ppermute(array, ("seq", "dp"), pairs)


def spread(x, w, u, k, pair_x, pair_u, far):
    batch = x.shape[0]
    proj, inner = project(x, w, u, k, w.shape[1])
    gp, *_ = early(x, w, u, k, pair_x, pair_u, far, proj, inner, 0, 0)
    input_grad = jnp.einsum("bpf,cf->bpc", gp, w, preferred_element_type=F32).astype(BF16)
    partial = lax.dot_general(x, gp, (((0, 1), (0, 1)), ((), ())), preferred_element_type=F32)
    over_seq = lax.psum_scatter(partial, "seq", scatter_dimension=1, tiled=True)
    total = lax.psum_scatter(over_seq, "dp", scatter_dimension=0, tiled=True)
    return input_grad, total / (batch * lax.axis_size("dp"))


def on_device(skip_input, upstream, proj_weight, depth_kernel):
    batch, rows, chans = skip_input.shape
    feats = upstream.shape[2]
    n_seq, n_dp = lax.axis_size("seq"), lax.axis_size("dp")
    seq, dee = lax.axis_index("seq"), lax.axis_index("dp")
    core, zed = seq % 2, seq // 2
    strip = feats // n_seq
    strips = n_seq // 4
    ncol = feats // 2

    there = functools.partial(pltpu.with_memory_space_constraint, memory_space=pltpu.HBM)
    x, w, u, k = skip_input, proj_weight, upstream, depth_kernel
    pair_x = lax.ppermute(x, "seq", near_pairs())
    pair_u = lax.ppermute(u, "seq", near_pairs())
    far = lax.ppermute(relay(edges(there(x), there(u))), "seq", far_pairs())
    if n_seq != 8 or n_dp != 4 or chans != 4 * (LANES + LANES // 2):
        return spread(x, w, u, k, pair_x, pair_u, far)
    proj, inner = project(x, w, u, k, ncol)
    gp_a, halo, halo_u, mine_a, send_a = early(x, w, u, k, pair_x, pair_u, far, proj, inner, strips, strip)
    got_a = lax.ppermute(send_a, "seq", near_pairs())
    gp_b, mine_b, send_b = late(u, k, proj, halo, halo_u, ncol, feats - ncol, strips, strip)
    got_b = lax.ppermute(send_b, "seq", near_pairs())
    blocks = pack(pair_x, got_b, *own(x, pair_x, mine_a, mine_b, got_a))

    input_grad, token = input_gradient(gp_a, gp_b, w)
    z_bits = [m * 2 * n_dp for m in range(4)]
    got = [exchange(blocks[i], *(FIRST[i][0], z_bits[FIRST[i][1]])) for i in (3, 2, 1)]
    own_block, *messages = fold([blocks] + got, token)
    got = [exchange(messages[k - 1], z_bits[k], k) for k in (3, 2, 1)]
    return input_grad, last([own_block] + got, 1.0 / (batch * n_dp))


def solution(mesh):
    return jax.shard_map(
        on_device,
        mesh=mesh,
        in_specs=(P("dp", "seq", None), P("dp", "seq", None), P(), P()),
        out_specs=(P("dp", "seq", None), P("dp", "seq")),
        check_vma=False,
    )
```

```python
import functools
import math

import jax
import jax.numpy as jnp
from jax import lax
from jax.experimental import pallas as pl
from jax.experimental.pallas import tpu as pltpu
from jax.sharding import PartitionSpec as P

BF16 = jnp.bfloat16
F32 = jnp.float32
C0 = math.sqrt(2.0 / math.pi)
ALPHA = (0.044715 * C0) ** (1.0 / 3.0)
KAPPA = C0 / ALPHA
LANES = 128
SUB = 8
PAD = 8
HOP = 9
FIRST = ((0, 0), (3, 2), (1, 1), (2, 3))
VMEM_BYTES = 14 * 1024 * 1024


def position():
    seq = lax.axis_index("seq")
    return lax.rem(seq, 2), lax.div(seq, 2), lax.axis_index("dp")


def vmem(count):
    return [pl.BlockSpec(memory_space=pltpu.VMEM)] * count


def params():
    return pltpu.CompilerParams(vmem_limit_bytes=VMEM_BYTES)


def shape(dims, dtype):
    return pltpu.VMEM(dims, dtype)


def here(array):
    return pltpu.with_memory_space_constraint(array, pltpu.VMEM)


def edges_kernel(x_ref, u_ref, far_ref, x_rows, u_rows, sems):
    batch, rows, chans = x_ref.shape
    even = position()[0] == 0
    start = pl.multiple_of(jnp.where(even, 0, rows - 16), 16)
    copies = [
        pltpu.make_async_copy(src.at[:, pl.ds(start, 16), :], dst, sems.at[i])
        for i, (src, dst) in enumerate(((x_ref, x_rows), (u_ref, u_rows)))
    ]
    for copy in copies:
        copy.start()
    for copy in copies:
        copy.wait()
    for held, lo, hi in ((x_rows, 0, chans), (u_rows, chans, far_ref.shape[1])):
        wide = [held[b].astype(F32) for b in range(batch)]
        wide = jnp.concatenate([jnp.where(even, one[:2], one[14:]) for one in wide], axis=0)
        far_ref[:, lo:hi] = wide.astype(BF16)


def edges(x, u):
    batch, _, chans = x.shape
    feats = u.shape[2]
    return pl.pallas_call(
        edges_kernel,
        out_shape=shape((2 * batch, chans + feats), BF16),
        in_specs=[pl.BlockSpec(memory_space=pltpu.HBM)] * 2,
        out_specs=vmem(1)[0],
        scratch_shapes=[pltpu.VMEM((batch, 16, chans), BF16), pltpu.VMEM((batch, 16, feats), BF16),
                        pltpu.SemaphoreType.DMA((2,))],
        compiler_params=params(),
        cost_estimate=pl.CostEstimate(flops=0, bytes_accessed=1_000, transcendentals=0),
        name="edges",
    )(x, u)


def relay_kernel(far_ref, far_out):
    far_out[...] = far_ref[...]


def relay(far):
    return pl.pallas_call(
        relay_kernel,
        out_shape=shape(far.shape, BF16),
        in_specs=vmem(1),
        out_specs=vmem(1)[0],
        compiler_params=params(),
        cost_estimate=pl.CostEstimate(flops=10_000_000_000, bytes_accessed=1_000_000, transcendentals=0),
        name="relay",
    )(here(far))


def slope(w):
    w2 = w * w
    t = jnp.tanh(w * (w2 + KAPPA))
    return (1.0 + t) * (w * (w2 + KAPPA / 3.0) * (1.0 - t) + 1.0 / 3.0)


def tap_sets(taps):
    k_sum, k_dif, k_mid = 0.5 * (taps[0:1] + taps[2:3]), 0.5 * (taps[0:1] - taps[2:3]), taps[1:2]
    return (ALPHA * taps[0:1], ALPHA * taps[1:2], ALPHA * taps[2:3]), (0.75 * k_sum, 0.75 * k_dif, 0.75 * k_mid)


def products(scaled, value):
    return [tap * value for tap in scaled]


def slopes(before, centre, after, u):
    fwd = slope(centre[1] + before[0] + after[2])
    rev = slope(centre[1] + before[2] + after[0])
    return u * (fwd + rev), u * (fwd - rev)


def inner_gradients(j, proj, u_ref, k_ref, wide, out, gp_ref, gp_lane):
    batch, rows = u_ref.shape[:2]
    seg = rows // SUB
    pitch = seg + PAD
    lanes = slice(j * LANES, (j + 1) * LANES)
    scaled, (g_sum, g_dif, g_mid) = tap_sets(k_ref[:, lanes])
    for b in range(batch):
        for s in range(SUB):
            wide[b, s * pitch:s * pitch + seg] = u_ref[b, s * seg:(s + 1) * seg, lanes].astype(F32)
    for b in range(batch):
        def vector(i, b=b):
            return products(scaled, proj[j, b, pl.ds(i, SUB, stride=pitch), :])

        def put(i, before, centre, after, dif_before, dif_after, b=b):
            out[b, i * HOP:i * HOP + SUB, :] = (
                g_mid * centre + g_sum * (before + after) + g_dif * (dif_after - dif_before))

        head, tail = vector(0), vector(seg - 1)
        before, stop = [pltpu.roll(one, 1, 0) for one in tail], [pltpu.roll(one, SUB - 1, 0) for one in head]
        sums, difs = [], []
        centre = head
        for i in range(seg):
            after = stop if i == seg - 1 else (tail if i == seg - 2 else vector(i + 1))
            one, two = slopes(before, centre, after, wide[b, pl.ds(i, SUB, stride=pitch), :])
            sums.append(one)
            difs.append(two)
            before, centre = centre, after
            if i >= 2:
                put(i - 1, sums[i - 2], sums[i - 1], sums[i], difs[i - 2], difs[i])
        put(0, pltpu.roll(sums[-1], 1, 0), sums[0], sums[1], pltpu.roll(difs[-1], 1, 0), difs[1])
        put(seg - 1, sums[-2], sums[-1], pltpu.roll(sums[0], SUB - 1, 0), difs[-2], pltpu.roll(difs[0], SUB - 1, 0))
        done = jnp.concatenate(
            [out[b, pl.ds(lo * HOP + s, SUB, stride=HOP), :] for s in range(SUB) for lo in range(0, seg, SUB)], axis=0)
        gp_ref[b, :, gp_lane:gp_lane + LANES] = done.astype(BF16)


def project_kernel(x_ref, w_ref, u_ref, k_ref, proj, gp_ref, wide, out):
    batch, rows, _ = x_ref.shape
    seg = rows // SUB
    pitch = seg + PAD
    tiles = gp_ref.shape[2] // LANES
    for b in range(batch):
        body = jnp.dot(x_ref[b], w_ref[...], preferred_element_type=F32).astype(BF16).astype(F32)
        for j in range(proj.shape[0]):
            for s in range(SUB):
                proj[j, b, s * pitch:s * pitch + seg] = body[s * seg:(s + 1) * seg, j * LANES:(j + 1) * LANES]
    for j in range(tiles):
        inner_gradients(j, proj, u_ref, k_ref, wide, out, gp_ref, j * LANES)


def pitched(rows):
    seg = rows // SUB
    return SUB * (seg + PAD) + seg


def sample_scratch(batch, rows):
    return [pltpu.VMEM((batch, pitched(rows), LANES), F32), pltpu.VMEM((batch, rows // SUB * HOP + 2 * SUB, LANES), F32)]


def project(x, w, u, k, ncol):
    batch, rows, _ = x.shape
    feats = w.shape[1]
    return pl.pallas_call(
        project_kernel,
        out_shape=[shape((feats // LANES, batch, pitched(rows), LANES), F32), shape((batch, rows, ncol), BF16)],
        in_specs=vmem(4),
        out_specs=vmem(2),
        scratch_shapes=sample_scratch(batch, rows),
        compiler_params=params(),
        cost_estimate=pl.CostEstimate(flops=4_000_000_000, bytes_accessed=4_000_000, transcendentals=0),
        name="project",
    )(*map(here, (x, w, u, k)))


def around(low, high):
    return jnp.concatenate([low, jnp.zeros((SUB - 4, low.shape[1]), low.dtype), high], axis=0)


def halo_of(pair_ref, far_rows):
    batch, rows, _ = pair_ref.shape
    even = position()[0] == 0
    far_rows = far_rows.astype(F32)
    result = []
    for b in range(batch):
        far = far_rows[2 * b:2 * b + 2]
        low, high = pair_ref[b, rows - 16:rows].astype(F32)[14:], pair_ref[b, 0:16].astype(F32)[:2]
        result.append(around(jnp.where(even, far, low), jnp.where(even, high, far)))
    return result


def finish(j, proj, u_ref, k_ref, halo_p, halo_u, inner_ref, gp_ref, gp_lane, gpt):
    batch, rows = u_ref.shape[:2]
    seg = rows // SUB
    pitch = seg + PAD
    lanes = slice(j * LANES, (j + 1) * LANES)
    cols = slice(gp_lane, gp_lane + LANES)
    scaled, (g_sum, g_dif, g_mid) = tap_sets(k_ref[:, lanes])
    sub = lax.broadcasted_iota(jnp.int32, (SUB, LANES), 0)

    def centred(low, high, halo):
        ends = jnp.where(sub == 0, pltpu.roll(halo, SUB - 1, 0), pltpu.roll(halo, 1, 0))
        inside = jnp.where(sub < 4, pltpu.roll(low, 1, 0), pltpu.roll(high, SUB - 1, 0))
        return jnp.where(jnp.logical_or(sub == 0, sub == SUB - 1), ends, inside)

    for b in range(batch):
        low = proj[j, b, 0:SUB]
        high = proj[j, b, (SUB - 1) * pitch + seg - SUB:(SUB - 1) * pitch + seg]
        halo = halo_p[b][:, lanes]
        before = jnp.where(sub < 2, halo, jnp.where(sub < 4, pltpu.roll(low, 2, 0), high))
        after = jnp.where(sub < 4, low, jnp.where(sub < 6, pltpu.roll(high, SUB - 2, 0), halo))
        u_low = u_ref[b, 0:16, lanes].astype(F32)[:SUB]
        u_high = u_ref[b, rows - 16:rows, lanes].astype(F32)[16 - SUB:]
        u = centred(u_low, u_high, halo_u[b][:, lanes])
        sums, difs = slopes(*(products(scaled, one) for one in (before, centred(low, high, halo), after)), u)
        ends = (g_mid * sums + g_sum * (pltpu.roll(sums, 1, 0) + pltpu.roll(sums, SUB - 1, 0))
                + g_dif * (pltpu.roll(difs, SUB - 1, 0) - pltpu.roll(difs, 1, 0)))
        first = inner_ref[b, 0:16, cols].astype(F32)
        last_rows = inner_ref[b, rows - 16:rows, cols].astype(F32)
        first = jnp.concatenate([jnp.where(sub < 2, pltpu.roll(ends, SUB - 1, 0), first[:SUB]), first[SUB:]], axis=0)
        last_rows = jnp.concatenate(
            [last_rows[:SUB], jnp.where(sub >= 6, pltpu.roll(ends, 1, 0), last_rows[SUB:])], axis=0)
        gp_ref[b, 0:16, cols] = first.astype(BF16)
        gp_ref[b, rows - 16:rows, cols] = last_rows.astype(BF16)
        if inner_ref is not gp_ref:
            gp_ref[b, 16:rows - 16, cols] = inner_ref[b, 16:rows - 16, cols]
        gpt[cols, b * rows:(b + 1) * rows] = gp_ref[b, :, cols].T


def hand_out(core, gpt, mine_ref, send_ref):
    strip = mine_ref.shape[1]
    for z in range(mine_ref.shape[0]):
        for result, who in ((mine_ref, core), (send_ref, 1 - core)):
            result[z] = gpt[pl.ds(pl.multiple_of((2 * z + who) * strip, 16), strip), :]


def early_kernel(
    x_ref, w_ref, u_ref, k_ref, pair_x, pair_u, far_ref, proj, inner_ref,
    gp_ref, halo_ref, halo_u_ref, *rest,
):
    *parts, gpt = rest
    batch, rows, chans = x_ref.shape
    halo_x = halo_of(pair_x, far_ref[:, :chans])
    halo_u = halo_of(pair_u, far_ref[:, chans:])
    for b in range(batch):
        halo_u_ref[b] = halo_u[b]
    halo_x = jnp.concatenate(halo_x, axis=0).astype(BF16)
    halo_all = jnp.dot(halo_x, w_ref[...], preferred_element_type=F32).astype(BF16).astype(F32)
    for b in range(batch):
        halo_ref[b] = halo_all[b * SUB:(b + 1) * SUB]
    halo_p = [halo_all[b * SUB:(b + 1) * SUB] for b in range(batch)]
    for j in range(gp_ref.shape[2] // LANES):
        finish(j, proj, u_ref, k_ref, halo_p, halo_u, inner_ref, gp_ref, j * LANES, gpt)
    if parts:
        hand_out(position()[0], gpt, *parts)


def late_kernel(
    col, u_ref, k_ref, proj, halo_ref, halo_u_ref,
    gp_ref, mine_ref, send_ref, wide, out, gpt,
):
    batch, rows, feats = u_ref.shape
    halo_u = [halo_u_ref[b] for b in range(batch)]
    halo_p = [halo_ref[b] for b in range(batch)]
    for t in range(gp_ref.shape[2] // LANES):
        j = col // LANES + t
        inner_gradients(j, proj, u_ref, k_ref, wide, out, gp_ref, t * LANES)
        finish(j, proj, u_ref, k_ref, halo_p, halo_u, gp_ref, gp_ref, t * LANES, gpt)
    hand_out(position()[0], gpt, mine_ref, send_ref)


def early(x, w, u, k, pair_x, pair_u, far, proj, inner, strips, strip):
    batch, rows, _ = x.shape
    ncol = inner.shape[2]
    parts = [shape((strips, strip, batch * rows), BF16)] * 2 if strips else []
    return pl.pallas_call(
        early_kernel,
        out_shape=[shape(inner.shape, BF16)] + [shape((batch, SUB, w.shape[1]), F32)] * 2 + parts,
        in_specs=vmem(9),
        out_specs=vmem(3 + len(parts)),
        scratch_shapes=[pltpu.VMEM((ncol, batch * rows), BF16)],
        compiler_params=params(),
        cost_estimate=pl.CostEstimate(flops=1_000_000_000, bytes_accessed=4_000_000, transcendentals=0),
        name="early",
    )(*map(here, (x, w, u, k, pair_x, pair_u, far, proj, inner)))


def late(u, k, proj, halo, halo_u, col, ncol, strips, strip):
    batch, rows, _ = u.shape
    part = shape((strips, strip, batch * rows), BF16)
    return pl.pallas_call(
        functools.partial(late_kernel, col),
        out_shape=[shape((batch, rows, ncol), BF16), part, part],
        in_specs=vmem(5),
        out_specs=vmem(3),
        scratch_shapes=sample_scratch(batch, rows) + [pltpu.VMEM((ncol, batch * rows), BF16)],
        compiler_params=params(),
        cost_estimate=pl.CostEstimate(flops=4_000_000_000, bytes_accessed=4_000_000, transcendentals=0),
        name="late",
    )(*map(here, (u, k, proj, halo, halo_u)))


def stacked(ref):
    return ref[...].reshape(ref.shape[0] * ref.shape[1], ref.shape[2])


def place_blocks(strips, sums_ref, out_ref):
    core, zed, dee = position()
    strip = sums_ref.shape[1]
    half = strip // 2
    left = lax.broadcasted_iota(jnp.int32, (half, LANES), 1) < LANES // 2

    def slot(turn, turns):
        return sum(jnp.where(turn == one, at, 0) for at, one in enumerate(turns))

    for z in strips:
        z_slot = slot(jnp.bitwise_xor(zed, z), [pair[1] for pair in FIRST])
        for b in range(4):
            b_slot = slot(jnp.bitwise_xor(dee, b), [pair[0] for pair in FIRST])
            at, spot = jnp.where(core == 0, b_slot, z_slot), jnp.where(core == 0, z, b)
            full = (3 * (b // 2) + 2 * (b % 2)) * LANES
            rest = (3 * (b // 2) + 1) * LANES
            top, bottom = sums_ref[z, 0:half, rest:rest + LANES], sums_ref[z, half:strip, rest:rest + LANES]
            if b % 2 == 0:
                packed = jnp.where(left, top, pltpu.roll(bottom, LANES // 2, 1))
            else:
                packed = jnp.where(left, pltpu.roll(top, LANES // 2, 1), bottom)
            out_ref[at, spot, 0:strip] = sums_ref[z, :, full:full + LANES].astype(BF16)
            out_ref[at, spot, strip:strip + half] = packed.astype(BF16)


def own_kernel(x_ref, other_ref, mine_a, mine_b, got_a, sums_ref, out_ref):
    flat, other = stacked(x_ref), stacked(other_ref)
    half, strip, _ = mine_a.shape
    later = jnp.dot(stacked(mine_b), flat, preferred_element_type=F32)
    sooner = (jnp.dot(stacked(mine_a), flat, preferred_element_type=F32)
              + jnp.dot(stacked(got_a), other, preferred_element_type=F32))
    for z in range(half):
        sums_ref[half + z] = later[z * strip:(z + 1) * strip]
        sums_ref[z] = sooner[z * strip:(z + 1) * strip]
    place_blocks(range(half), sums_ref, out_ref)


def own(x, other, mine_a, mine_b, got_a):
    half, strip, _ = mine_a.shape
    return pl.pallas_call(
        own_kernel,
        out_shape=[shape((2 * half, strip, x.shape[2]), F32), shape((4, 4, strip + strip // 2, LANES), BF16)],
        in_specs=vmem(5),
        out_specs=vmem(2),
        compiler_params=params(),
        cost_estimate=pl.CostEstimate(flops=1_000_000_000, bytes_accessed=4_000_000, transcendentals=0),
        name="own",
    )(*map(here, (x, other, mine_a, mine_b, got_a)))


def pack_kernel(other_ref, got_b, sums_in, blocks_in, sums_ref, out_ref):
    half, strip, _ = got_b.shape
    later = jnp.dot(stacked(got_b), stacked(other_ref), preferred_element_type=F32)
    for z in range(half):
        sums_ref[half + z] = sums_in[half + z] + later[z * strip:(z + 1) * strip]
    place_blocks(range(half, 2 * half), sums_ref, out_ref)


def pack(other, got_b, sums, blocks):
    return pl.pallas_call(
        pack_kernel,
        out_shape=[shape(sums.shape, F32), shape(blocks.shape, BF16)],
        in_specs=vmem(4),
        out_specs=vmem(2),
        input_output_aliases={2: 0, 3: 1},
        compiler_params=params(),
        name="pack",
    )(*map(here, (other, got_b, sums, blocks)))[1]


def fold_kernel(own_ref, one_ref, two_ref, three_ref, token, *outs):
    core, zed, dee = position()
    mine = jnp.where(core == 0, zed, dee)
    for k in (3, 2, 1, 0):
        j = jnp.bitwise_xor(mine, k)
        total = own_ref[0, j].astype(F32) + one_ref[j].astype(F32) + two_ref[j].astype(F32) + three_ref[j].astype(F32)
        outs[k][...] = total.astype(outs[k].dtype)


def fold(parts, token):
    block = parts[1].shape[1:]
    return pl.pallas_call(
        fold_kernel,
        out_shape=[shape(block, F32)] + [shape(block, BF16)] * 3,
        in_specs=vmem(5),
        out_specs=vmem(4),
        compiler_params=params(),
        name="fold",
    )(*map(here, parts), here(token))


def input_kernel(gp_a, gp_b, w_ref, out_ref, token):
    token[...] = jnp.zeros_like(token)
    cut = gp_a.shape[2]
    for b in range(out_ref.shape[0]):
        total = lax.dot_general(gp_a[b], w_ref[:, :cut], (((1,), (1,)), ((), ())), preferred_element_type=F32)
        total += lax.dot_general(gp_b[b], w_ref[:, cut:], (((1,), (1,)), ((), ())), preferred_element_type=F32)
        out_ref[b] = total.astype(BF16)


def input_gradient(gp_a, gp_b, w):
    batch, rows, _ = gp_a.shape
    return pl.pallas_call(
        input_kernel,
        out_shape=[jax.ShapeDtypeStruct((batch, rows, w.shape[0]), BF16), shape((SUB, LANES), F32)],
        in_specs=vmem(3),
        out_specs=vmem(2),
        compiler_params=params(),
        cost_estimate=pl.CostEstimate(flops=2_000_000_000, bytes_accessed=1_000_000, transcendentals=0),
        name="input_gradient",
    )(here(gp_a), here(gp_b), here(w))


def last_kernel(scale, own_ref, one_ref, two_ref, three_ref, out_ref):
    odd = lax.rem(position()[2], 2)
    total = own_ref[...] + one_ref[...].astype(F32) + two_ref[...].astype(F32) + three_ref[...].astype(F32)
    total = total * scale
    strip = out_ref.shape[0]
    half = LANES // 2
    full, rest = total[:strip], total[strip:]
    rest = jnp.concatenate([rest[:, :half], rest[:, half:]], axis=0)

    @pl.when(odd == 0)
    def _():
        out_ref[:, :LANES] = full
        out_ref[:, LANES:] = rest

    @pl.when(odd == 1)
    def _():
        out_ref[:, :half] = rest
        out_ref[:, half:] = full


def last(parts, scale):
    strip = parts[0].shape[0] * 2 // 3
    return pl.pallas_call(
        functools.partial(last_kernel, scale),
        out_shape=jax.ShapeDtypeStruct((strip, LANES + LANES // 2), F32),
        in_specs=vmem(4),
        out_specs=vmem(1)[0],
        compiler_params=params(),
        name="last",
    )(*parts).T


def near_pairs():
    count = lax.axis_size("seq")
    return [(i, i ^ 1) for i in range(count) if i ^ 1 < count]


def far_pairs():
    count = lax.axis_size("seq")
    pairs = [(i, i - 1 if i % 2 == 0 else i + 1) for i in range(count)]
    return [(a, b) for a, b in pairs if 0 <= b < count]


def exchange(array, one, two):
    n_seq, n_dp = lax.axis_size("seq"), lax.axis_size("dp")
    pairs = [(i, i ^ (two if (i // n_dp) % 2 else one)) for i in range(n_seq * n_dp)]
    return lax.ppermute(array, ("seq", "dp"), pairs)


def spread(x, w, u, k, pair_x, pair_u, far):
    batch = x.shape[0]
    proj, inner = project(x, w, u, k, w.shape[1])
    gp, *_ = early(x, w, u, k, pair_x, pair_u, far, proj, inner, 0, 0)
    input_grad = jnp.einsum("bpf,cf->bpc", gp, w, preferred_element_type=F32).astype(BF16)
    partial = lax.dot_general(x, gp, (((0, 1), (0, 1)), ((), ())), preferred_element_type=F32)
    over_seq = lax.psum_scatter(partial, "seq", scatter_dimension=1, tiled=True)
    total = lax.psum_scatter(over_seq, "dp", scatter_dimension=0, tiled=True)
    return input_grad, total / (batch * lax.axis_size("dp"))


def on_device(skip_input, upstream, proj_weight, depth_kernel):
    batch, rows, chans = skip_input.shape
    feats = upstream.shape[2]
    n_seq, n_dp = lax.axis_size("seq"), lax.axis_size("dp")
    seq, dee = lax.axis_index("seq"), lax.axis_index("dp")
    core, zed = seq % 2, seq // 2
    strip = feats // n_seq
    strips = n_seq // 4
    ncol = feats // 2

    there = functools.partial(pltpu.with_memory_space_constraint, memory_space=pltpu.HBM)
    x, w, u, k = skip_input, proj_weight, upstream, depth_kernel
    pair_x = lax.ppermute(x, "seq", near_pairs())
    pair_u = lax.ppermute(u, "seq", near_pairs())
    far = lax.ppermute(relay(edges(there(x), there(u))), "seq", far_pairs())
    if n_seq != 8 or n_dp != 4 or chans != 4 * (LANES + LANES // 2):
        return spread(x, w, u, k, pair_x, pair_u, far)
    proj, inner = project(x, w, u, k, ncol)
    gp_a, halo, halo_u, mine_a, send_a = early(x, w, u, k, pair_x, pair_u, far, proj, inner, strips, strip)
    got_a = lax.ppermute(send_a, "seq", near_pairs())
    gp_b, mine_b, send_b = late(u, k, proj, halo, halo_u, ncol, feats - ncol, strips, strip)
    got_b = lax.ppermute(send_b, "seq", near_pairs())
    blocks = pack(pair_x, got_b, *own(x, pair_x, mine_a, mine_b, got_a))

    input_grad, token = input_gradient(gp_a, gp_b, w)
    z_bits = [m * 2 * n_dp for m in range(4)]
    got = [exchange(blocks[i], *(FIRST[i][0], z_bits[FIRST[i][1]])) for i in (3, 2, 1)]
    own_block, *messages = fold([blocks] + got, token)
    got = [exchange(messages[k - 1], z_bits[k], k) for k in (3, 2, 1)]
    return input_grad, last([own_block] + got, 1.0 / (batch * n_dp))


def solution(mesh):
    return jax.shard_map(
        on_device,
        mesh=mesh,
        in_specs=(P("dp", "seq", None), P("dp", "seq", None), P(), P()),
        out_specs=(P("dp", "seq", None), P("dp", "seq")),
        check_vma=False,
    )
```

```python
import functools
import math

import jax
import jax.numpy as jnp
from jax import lax
from jax.experimental import pallas as pl
from jax.experimental.pallas import tpu as pltpu
from jax.sharding import PartitionSpec as P

BF16 = jnp.bfloat16
F32 = jnp.float32
C0 = math.sqrt(2.0 / math.pi)
ALPHA = (0.044715 * C0) ** (1.0 / 3.0)
KAPPA = C0 / ALPHA
LANES = 128
SUB = 8
PAD = 8
HOP = 9
FIRST = ((0, 0), (3, 2), (1, 1), (2, 3))
SECOND = ((0, 0), (3, 2), (2, 3), (1, 1))
VMEM_BYTES = 14 * 1024 * 1024


def position():
    seq = lax.axis_index("seq")
    return lax.rem(seq, 2), lax.div(seq, 2), lax.axis_index("dp")


def vmem(count):
    return [pl.BlockSpec(memory_space=pltpu.VMEM)] * count


def params():
    return pltpu.CompilerParams(vmem_limit_bytes=VMEM_BYTES)


def shape(dims, dtype):
    return pltpu.VMEM(dims, dtype)


def here(array):
    return pltpu.with_memory_space_constraint(array, pltpu.VMEM)


def edges_kernel(x_ref, u_ref, far_ref, x_rows, u_rows, sems):
    batch, rows, chans = x_ref.shape
    even = position()[0] == 0
    start = pl.multiple_of(jnp.where(even, 0, rows - 16), 16)
    copies = [
        pltpu.make_async_copy(src.at[:, pl.ds(start, 16), :], dst, sems.at[i])
        for i, (src, dst) in enumerate(((x_ref, x_rows), (u_ref, u_rows)))
    ]
    for copy in copies:
        copy.start()
    for copy in copies:
        copy.wait()
    for held, lo, hi in ((x_rows, 0, chans), (u_rows, chans, far_ref.shape[1])):
        wide = [held[b].astype(F32) for b in range(batch)]
        wide = jnp.concatenate([jnp.where(even, one[:2], one[14:]) for one in wide], axis=0)
        far_ref[:, lo:hi] = wide.astype(BF16)


def edges(x, u):
    batch, _, chans = x.shape
    feats = u.shape[2]
    return pl.pallas_call(
        edges_kernel,
        out_shape=shape((2 * batch, chans + feats), BF16),
        in_specs=[pl.BlockSpec(memory_space=pltpu.HBM)] * 2,
        out_specs=vmem(1)[0],
        scratch_shapes=[pltpu.VMEM((batch, 16, chans), BF16), pltpu.VMEM((batch, 16, feats), BF16),
                        pltpu.SemaphoreType.DMA((2,))],
        compiler_params=params(),
        cost_estimate=pl.CostEstimate(flops=0, bytes_accessed=1_000, transcendentals=0),
        name="edges",
    )(x, u)


def relay_kernel(far_ref, far_out):
    far_out[...] = far_ref[...]


def relay(far):
    return pl.pallas_call(
        relay_kernel,
        out_shape=shape(far.shape, BF16),
        in_specs=vmem(1),
        out_specs=vmem(1)[0],
        compiler_params=params(),
        cost_estimate=pl.CostEstimate(flops=10_000_000_000, bytes_accessed=1_000_000, transcendentals=0),
        name="relay",
    )(here(far))


def slope(w):
    w2 = w * w
    t = jnp.tanh(w * (w2 + KAPPA))
    return (1.0 + t) * (w * (w2 + KAPPA / 3.0) * (1.0 - t) + 1.0 / 3.0)


def tap_sets(taps):
    k_sum, k_dif, k_mid = 0.5 * (taps[0:1] + taps[2:3]), 0.5 * (taps[0:1] - taps[2:3]), taps[1:2]
    return (ALPHA * taps[0:1], ALPHA * taps[1:2], ALPHA * taps[2:3]), (0.75 * k_sum, 0.75 * k_dif, 0.75 * k_mid)


def products(scaled, value):
    return [tap * value for tap in scaled]


def slopes(before, centre, after, u):
    fwd = slope(centre[1] + before[0] + after[2])
    rev = slope(centre[1] + before[2] + after[0])
    return u * (fwd + rev), u * (fwd - rev)


def inner_gradients(j, proj, u_ref, k_ref, wide, out, gp_ref, gp_lane):
    batch, rows = u_ref.shape[:2]
    seg = rows // SUB
    pitch = seg + PAD
    lanes = slice(j * LANES, (j + 1) * LANES)
    scaled, (g_sum, g_dif, g_mid) = tap_sets(k_ref[:, lanes])
    for b in range(batch):
        for s in range(SUB):
            wide[b, s * pitch:s * pitch + seg] = u_ref[b, s * seg:(s + 1) * seg, lanes].astype(F32)
    for b in range(batch):
        def vector(i, b=b):
            return products(scaled, proj[j, b, pl.ds(i, SUB, stride=pitch), :])

        def put(i, before, centre, after, dif_before, dif_after, b=b):
            out[b, i * HOP:i * HOP + SUB, :] = (
                g_mid * centre + g_sum * (before + after) + g_dif * (dif_after - dif_before))

        head, tail = vector(0), vector(seg - 1)
        before, stop = [pltpu.roll(one, 1, 0) for one in tail], [pltpu.roll(one, SUB - 1, 0) for one in head]
        sums, difs = [], []
        centre = head
        for i in range(seg):
            after = stop if i == seg - 1 else (tail if i == seg - 2 else vector(i + 1))
            one, two = slopes(before, centre, after, wide[b, pl.ds(i, SUB, stride=pitch), :])
            sums.append(one)
            difs.append(two)
            before, centre = centre, after
            if i >= 2:
                put(i - 1, sums[i - 2], sums[i - 1], sums[i], difs[i - 2], difs[i])
        put(0, pltpu.roll(sums[-1], 1, 0), sums[0], sums[1], pltpu.roll(difs[-1], 1, 0), difs[1])
        put(seg - 1, sums[-2], sums[-1], pltpu.roll(sums[0], SUB - 1, 0), difs[-2], pltpu.roll(difs[0], SUB - 1, 0))
        done = jnp.concatenate(
            [out[b, pl.ds(lo * HOP + s, SUB, stride=HOP), :] for s in range(SUB) for lo in range(0, seg, SUB)], axis=0)
        gp_ref[b, :, gp_lane:gp_lane + LANES] = done.astype(BF16)


def project_kernel(x_ref, w_ref, u_ref, k_ref, proj, gp_ref, wide, out):
    batch, rows, _ = x_ref.shape
    seg = rows // SUB
    pitch = seg + PAD
    tiles = gp_ref.shape[2] // LANES
    for b in range(batch):
        body = jnp.dot(x_ref[b], w_ref[...], preferred_element_type=F32).astype(BF16).astype(F32)
        for j in range(proj.shape[0]):
            for s in range(SUB):
                proj[j, b, s * pitch:s * pitch + seg] = body[s * seg:(s + 1) * seg, j * LANES:(j + 1) * LANES]
    for j in range(tiles):
        inner_gradients(j, proj, u_ref, k_ref, wide, out, gp_ref, j * LANES)


def pitched(rows):
    seg = rows // SUB
    return SUB * (seg + PAD) + seg


def sample_scratch(batch, rows):
    return [pltpu.VMEM((batch, pitched(rows), LANES), F32), pltpu.VMEM((batch, rows // SUB * HOP + 2 * SUB, LANES), F32)]


def project(x, w, u, k, ncol):
    batch, rows, _ = x.shape
    feats = w.shape[1]
    return pl.pallas_call(
        project_kernel,
        out_shape=[shape((feats // LANES, batch, pitched(rows), LANES), F32), shape((batch, rows, ncol), BF16)],
        in_specs=vmem(4),
        out_specs=vmem(2),
        scratch_shapes=sample_scratch(batch, rows),
        compiler_params=params(),
        cost_estimate=pl.CostEstimate(flops=4_000_000_000, bytes_accessed=4_000_000, transcendentals=0),
        name="project",
    )(*map(here, (x, w, u, k)))


def around(low, high):
    return jnp.concatenate([low, jnp.zeros((SUB - 4, low.shape[1]), low.dtype), high], axis=0)


def halo_of(pair_ref, far_rows):
    batch, rows, _ = pair_ref.shape
    even = position()[0] == 0
    far_rows = far_rows.astype(F32)
    result = []
    for b in range(batch):
        far = far_rows[2 * b:2 * b + 2]
        low, high = pair_ref[b, rows - 16:rows].astype(F32)[14:], pair_ref[b, 0:16].astype(F32)[:2]
        result.append(around(jnp.where(even, far, low), jnp.where(even, high, far)))
    return result


def finish(j, proj, u_ref, k_ref, halo_p, halo_u, inner_ref, gp_ref, gp_lane, gpt):
    batch, rows = u_ref.shape[:2]
    seg = rows // SUB
    pitch = seg + PAD
    lanes = slice(j * LANES, (j + 1) * LANES)
    cols = slice(gp_lane, gp_lane + LANES)
    scaled, (g_sum, g_dif, g_mid) = tap_sets(k_ref[:, lanes])
    sub = lax.broadcasted_iota(jnp.int32, (SUB, LANES), 0)

    def centred(low, high, halo):
        ends = jnp.where(sub == 0, pltpu.roll(halo, SUB - 1, 0), pltpu.roll(halo, 1, 0))
        inside = jnp.where(sub < 4, pltpu.roll(low, 1, 0), pltpu.roll(high, SUB - 1, 0))
        return jnp.where(jnp.logical_or(sub == 0, sub == SUB - 1), ends, inside)

    for b in range(batch):
        low = proj[j, b, 0:SUB]
        high = proj[j, b, (SUB - 1) * pitch + seg - SUB:(SUB - 1) * pitch + seg]
        halo = halo_p[b][:, lanes]
        before = jnp.where(sub < 2, halo, jnp.where(sub < 4, pltpu.roll(low, 2, 0), high))
        after = jnp.where(sub < 4, low, jnp.where(sub < 6, pltpu.roll(high, SUB - 2, 0), halo))
        u_low = u_ref[b, 0:16, lanes].astype(F32)[:SUB]
        u_high = u_ref[b, rows - 16:rows, lanes].astype(F32)[16 - SUB:]
        u = centred(u_low, u_high, halo_u[b][:, lanes])
        sums, difs = slopes(*(products(scaled, one) for one in (before, centred(low, high, halo), after)), u)
        ends = (g_mid * sums + g_sum * (pltpu.roll(sums, 1, 0) + pltpu.roll(sums, SUB - 1, 0))
                + g_dif * (pltpu.roll(difs, SUB - 1, 0) - pltpu.roll(difs, 1, 0)))
        first = inner_ref[b, 0:16, cols].astype(F32)
        last_rows = inner_ref[b, rows - 16:rows, cols].astype(F32)
        first = jnp.concatenate([jnp.where(sub < 2, pltpu.roll(ends, SUB - 1, 0), first[:SUB]), first[SUB:]], axis=0)
        last_rows = jnp.concatenate(
            [last_rows[:SUB], jnp.where(sub >= 6, pltpu.roll(ends, 1, 0), last_rows[SUB:])], axis=0)
        gp_ref[b, 0:16, cols] = first.astype(BF16)
        gp_ref[b, rows - 16:rows, cols] = last_rows.astype(BF16)
        if inner_ref is not gp_ref:
            gp_ref[b, 16:rows - 16, cols] = inner_ref[b, 16:rows - 16, cols]
        gpt[cols, b * rows:(b + 1) * rows] = gp_ref[b, :, cols].T


def hand_out(core, gpt, mine_ref, send_ref):
    strip = mine_ref.shape[1]
    for z in range(mine_ref.shape[0]):
        for result, who in ((mine_ref, core), (send_ref, 1 - core)):
            result[z] = gpt[pl.ds(pl.multiple_of((2 * z + who) * strip, 16), strip), :]


def early_kernel(
    x_ref, w_ref, u_ref, k_ref, pair_x, pair_u, far_ref, proj, inner_ref,
    gp_ref, halo_ref, halo_u_ref, *rest,
):
    *parts, gpt = rest
    batch, rows, chans = x_ref.shape
    halo_x = halo_of(pair_x, far_ref[:, :chans])
    halo_u = halo_of(pair_u, far_ref[:, chans:])
    for b in range(batch):
        halo_u_ref[b] = halo_u[b]
    halo_x = jnp.concatenate(halo_x, axis=0).astype(BF16)
    halo_all = jnp.dot(halo_x, w_ref[...], preferred_element_type=F32).astype(BF16).astype(F32)
    for b in range(batch):
        halo_ref[b] = halo_all[b * SUB:(b + 1) * SUB]
    halo_p = [halo_all[b * SUB:(b + 1) * SUB] for b in range(batch)]
    for j in range(gp_ref.shape[2] // LANES):
        finish(j, proj, u_ref, k_ref, halo_p, halo_u, inner_ref, gp_ref, j * LANES, gpt)
    if parts:
        hand_out(position()[0], gpt, *parts)


def late_kernel(
    col, u_ref, k_ref, proj, halo_ref, halo_u_ref,
    gp_ref, mine_ref, send_ref, wide, out, gpt,
):
    batch, rows, feats = u_ref.shape
    halo_u = [halo_u_ref[b] for b in range(batch)]
    halo_p = [halo_ref[b] for b in range(batch)]
    for t in range(gp_ref.shape[2] // LANES):
        j = col // LANES + t
        inner_gradients(j, proj, u_ref, k_ref, wide, out, gp_ref, t * LANES)
        finish(j, proj, u_ref, k_ref, halo_p, halo_u, gp_ref, gp_ref, t * LANES, gpt)
    hand_out(position()[0], gpt, mine_ref, send_ref)


def early(x, w, u, k, pair_x, pair_u, far, proj, inner, strips, strip):
    batch, rows, _ = x.shape
    ncol = inner.shape[2]
    parts = [shape((strips, strip, batch * rows), BF16)] * 2 if strips else []
    return pl.pallas_call(
        early_kernel,
        out_shape=[shape(inner.shape, BF16)] + [shape((batch, SUB, w.shape[1]), F32)] * 2 + parts,
        in_specs=vmem(9),
        out_specs=vmem(3 + len(parts)),
        scratch_shapes=[pltpu.VMEM((ncol, batch * rows), BF16)],
        compiler_params=params(),
        cost_estimate=pl.CostEstimate(flops=1_000_000_000, bytes_accessed=4_000_000, transcendentals=0),
        name="early",
    )(*map(here, (x, w, u, k, pair_x, pair_u, far, proj, inner)))


def late(u, k, proj, halo, halo_u, col, ncol, strips, strip):
    batch, rows, _ = u.shape
    part = shape((strips, strip, batch * rows), BF16)
    return pl.pallas_call(
        functools.partial(late_kernel, col),
        out_shape=[shape((batch, rows, ncol), BF16), part, part],
        in_specs=vmem(5),
        out_specs=vmem(3),
        scratch_shapes=sample_scratch(batch, rows) + [pltpu.VMEM((ncol, batch * rows), BF16)],
        compiler_params=params(),
        cost_estimate=pl.CostEstimate(flops=4_000_000_000, bytes_accessed=4_000_000, transcendentals=0),
        name="late",
    )(*map(here, (u, k, proj, halo, halo_u)))


def stacked(ref):
    return ref[...].reshape(ref.shape[0] * ref.shape[1], ref.shape[2])


def place_blocks(strips, sums_ref, out_ref):
    core, zed, dee = position()
    strip = sums_ref.shape[1]
    half = strip // 2
    left = lax.broadcasted_iota(jnp.int32, (half, LANES), 1) < LANES // 2

    def slot(turn, turns):
        return sum(jnp.where(turn == one, at, 0) for at, one in enumerate(turns))

    for z in strips:
        z_slot = slot(jnp.bitwise_xor(zed, z), [pair[1] for pair in FIRST])
        for b in range(4):
            b_slot = slot(jnp.bitwise_xor(dee, b), [pair[0] for pair in FIRST])
            at, spot = jnp.where(core == 0, b_slot, z_slot), jnp.where(core == 0, z, b)
            full = (3 * (b // 2) + 2 * (b % 2)) * LANES
            rest = (3 * (b // 2) + 1) * LANES
            top, bottom = sums_ref[z, 0:half, rest:rest + LANES], sums_ref[z, half:strip, rest:rest + LANES]
            if b % 2 == 0:
                packed = jnp.where(left, top, pltpu.roll(bottom, LANES // 2, 1))
            else:
                packed = jnp.where(left, pltpu.roll(top, LANES // 2, 1), bottom)
            out_ref[at, spot, 0:strip] = sums_ref[z, :, full:full + LANES].astype(BF16)
            out_ref[at, spot, strip:strip + half] = packed.astype(BF16)


def own_kernel(x_ref, other_ref, mine_a, mine_b, got_a, sums_ref, out_ref):
    flat, other = stacked(x_ref), stacked(other_ref)
    half, strip, _ = mine_a.shape
    later = jnp.dot(stacked(mine_b), flat, preferred_element_type=F32)
    sooner = (jnp.dot(stacked(mine_a), flat, preferred_element_type=F32)
              + jnp.dot(stacked(got_a), other, preferred_element_type=F32))
    for z in range(half):
        sums_ref[half + z] = later[z * strip:(z + 1) * strip]
        sums_ref[z] = sooner[z * strip:(z + 1) * strip]
    place_blocks(range(half), sums_ref, out_ref)


def own(x, other, mine_a, mine_b, got_a):
    half, strip, _ = mine_a.shape
    return pl.pallas_call(
        own_kernel,
        out_shape=[shape((2 * half, strip, x.shape[2]), F32), shape((4, 4, strip + strip // 2, LANES), BF16)],
        in_specs=vmem(5),
        out_specs=vmem(2),
        compiler_params=params(),
        cost_estimate=pl.CostEstimate(flops=1_000_000_000, bytes_accessed=4_000_000, transcendentals=0),
        name="own",
    )(*map(here, (x, other, mine_a, mine_b, got_a)))


def pack_kernel(other_ref, got_b, sums_in, blocks_in, sums_ref, out_ref):
    half, strip, _ = got_b.shape
    later = jnp.dot(stacked(got_b), stacked(other_ref), preferred_element_type=F32)
    for z in range(half):
        sums_ref[half + z] = sums_in[half + z] + later[z * strip:(z + 1) * strip]
    place_blocks(range(half, 2 * half), sums_ref, out_ref)


def pack(other, got_b, sums, blocks):
    return pl.pallas_call(
        pack_kernel,
        out_shape=[shape(sums.shape, F32), shape(blocks.shape, BF16)],
        in_specs=vmem(4),
        out_specs=vmem(2),
        input_output_aliases={2: 0, 3: 1},
        compiler_params=params(),
        name="pack",
    )(*map(here, (other, got_b, sums, blocks)))[1]


def fold_kernel(own_ref, one_ref, two_ref, three_ref, token, *outs):
    core, zed, dee = position()
    for (z_turn, d_turn), out in zip(SECOND, outs):
        j = jnp.where(core == 0, jnp.bitwise_xor(zed, z_turn), jnp.bitwise_xor(dee, d_turn))
        total = own_ref[0, j].astype(F32) + one_ref[j].astype(F32) + two_ref[j].astype(F32) + three_ref[j].astype(F32)
        out[...] = total.astype(out.dtype)


def fold(parts, token):
    block = parts[1].shape[1:]
    return pl.pallas_call(
        fold_kernel,
        out_shape=[shape(block, F32)] + [shape(block, BF16)] * 3,
        in_specs=vmem(5),
        out_specs=vmem(4),
        compiler_params=params(),
        name="fold",
    )(*map(here, parts), here(token))


def input_kernel(gp_a, gp_b, w_ref, out_ref, token):
    token[...] = jnp.zeros_like(token)
    cut = gp_a.shape[2]
    for b in range(out_ref.shape[0]):
        total = lax.dot_general(gp_a[b], w_ref[:, :cut], (((1,), (1,)), ((), ())), preferred_element_type=F32)
        total += lax.dot_general(gp_b[b], w_ref[:, cut:], (((1,), (1,)), ((), ())), preferred_element_type=F32)
        out_ref[b] = total.astype(BF16)


def input_gradient(gp_a, gp_b, w):
    batch, rows, _ = gp_a.shape
    return pl.pallas_call(
        input_kernel,
        out_shape=[jax.ShapeDtypeStruct((batch, rows, w.shape[0]), BF16), shape((SUB, LANES), F32)],
        in_specs=vmem(3),
        out_specs=vmem(2),
        compiler_params=params(),
        cost_estimate=pl.CostEstimate(flops=2_000_000_000, bytes_accessed=1_000_000, transcendentals=0),
        name="input_gradient",
    )(here(gp_a), here(gp_b), here(w))


def last_kernel(scale, own_ref, one_ref, two_ref, three_ref, out_ref):
    odd = lax.rem(position()[2], 2)
    total = own_ref[...] + one_ref[...].astype(F32) + two_ref[...].astype(F32) + three_ref[...].astype(F32)
    total = total * scale
    strip = out_ref.shape[0]
    half = LANES // 2
    full, rest = total[:strip], total[strip:]
    rest = jnp.concatenate([rest[:, :half], rest[:, half:]], axis=0)

    @pl.when(odd == 0)
    def _():
        out_ref[:, :LANES] = full
        out_ref[:, LANES:] = rest

    @pl.when(odd == 1)
    def _():
        out_ref[:, :half] = rest
        out_ref[:, half:] = full


def last(parts, scale):
    strip = parts[0].shape[0] * 2 // 3
    return pl.pallas_call(
        functools.partial(last_kernel, scale),
        out_shape=jax.ShapeDtypeStruct((strip, LANES + LANES // 2), F32),
        in_specs=vmem(4),
        out_specs=vmem(1)[0],
        compiler_params=params(),
        name="last",
    )(*parts).T


def near_pairs():
    count = lax.axis_size("seq")
    return [(i, i ^ 1) for i in range(count) if i ^ 1 < count]


def far_pairs():
    count = lax.axis_size("seq")
    pairs = [(i, i - 1 if i % 2 == 0 else i + 1) for i in range(count)]
    return [(a, b) for a, b in pairs if 0 <= b < count]


def exchange(array, one, two):
    n_seq, n_dp = lax.axis_size("seq"), lax.axis_size("dp")
    pairs = [(i, i ^ (two if (i // n_dp) % 2 else one)) for i in range(n_seq * n_dp)]
    return lax.ppermute(array, ("seq", "dp"), pairs)


def spread(x, w, u, k, pair_x, pair_u, far):
    batch = x.shape[0]
    proj, inner = project(x, w, u, k, w.shape[1])
    gp, *_ = early(x, w, u, k, pair_x, pair_u, far, proj, inner, 0, 0)
    input_grad = jnp.einsum("bpf,cf->bpc", gp, w, preferred_element_type=F32).astype(BF16)
    partial = lax.dot_general(x, gp, (((0, 1), (0, 1)), ((), ())), preferred_element_type=F32)
    over_seq = lax.psum_scatter(partial, "seq", scatter_dimension=1, tiled=True)
    total = lax.psum_scatter(over_seq, "dp", scatter_dimension=0, tiled=True)
    return input_grad, total / (batch * lax.axis_size("dp"))


def on_device(skip_input, upstream, proj_weight, depth_kernel):
    batch, rows, chans = skip_input.shape
    feats = upstream.shape[2]
    n_seq, n_dp = lax.axis_size("seq"), lax.axis_size("dp")
    seq, dee = lax.axis_index("seq"), lax.axis_index("dp")
    core, zed = seq % 2, seq // 2
    strip = feats // n_seq
    strips = n_seq // 4
    ncol = feats // 2

    there = functools.partial(pltpu.with_memory_space_constraint, memory_space=pltpu.HBM)
    x, w, u, k = skip_input, proj_weight, upstream, depth_kernel
    pair_x = lax.ppermute(x, "seq", near_pairs())
    pair_u = lax.ppermute(u, "seq", near_pairs())
    far = lax.ppermute(relay(edges(there(x), there(u))), "seq", far_pairs())
    if n_seq != 8 or n_dp != 4 or chans != 4 * (LANES + LANES // 2):
        return spread(x, w, u, k, pair_x, pair_u, far)
    proj, inner = project(x, w, u, k, ncol)
    gp_a, halo, halo_u, mine_a, send_a = early(x, w, u, k, pair_x, pair_u, far, proj, inner, strips, strip)
    got_a = lax.ppermute(send_a, "seq", near_pairs())
    gp_b, mine_b, send_b = late(u, k, proj, halo, halo_u, ncol, feats - ncol, strips, strip)
    got_b = lax.ppermute(send_b, "seq", near_pairs())
    blocks = pack(pair_x, got_b, *own(x, pair_x, mine_a, mine_b, got_a))

    input_grad, token = input_gradient(gp_a, gp_b, w)
    z_bits = [m * 2 * n_dp for m in range(4)]
    got = [exchange(blocks[i], *(FIRST[i][0], z_bits[FIRST[i][1]])) for i in (3, 2, 1)]
    own_block, *messages = fold([blocks] + got, token)
    got = [exchange(message, z_bits[z], d) for message, (z, d) in zip(messages, SECOND[1:])]
    return input_grad, last([own_block] + got, 1.0 / (batch * n_dp))


def solution(mesh):
    return jax.shard_map(
        on_device,
        mesh=mesh,
        in_specs=(P("dp", "seq", None), P("dp", "seq", None), P(), P()),
        out_specs=(P("dp", "seq", None), P("dp", "seq")),
        check_vma=False,
    )
```

```python
import functools
import math

import jax
import jax.numpy as jnp
from jax import lax
from jax.experimental import pallas as pl
from jax.experimental.pallas import tpu as pltpu
from jax.sharding import PartitionSpec as P

BF16 = jnp.bfloat16
F32 = jnp.float32
C0 = math.sqrt(2.0 / math.pi)
ALPHA = (0.044715 * C0) ** (1.0 / 3.0)
KAPPA = C0 / ALPHA
LANES = 128
SUB = 8
PAD = 8
HOP = 9
FIRST = ((0, 0), (3, 2), (2, 3), (1, 1))
VMEM_BYTES = 14 * 1024 * 1024


def position():
    seq = lax.axis_index("seq")
    return lax.rem(seq, 2), lax.div(seq, 2), lax.axis_index("dp")


def vmem(count):
    return [pl.BlockSpec(memory_space=pltpu.VMEM)] * count


def params():
    return pltpu.CompilerParams(vmem_limit_bytes=VMEM_BYTES)


def shape(dims, dtype):
    return pltpu.VMEM(dims, dtype)


def here(array):
    return pltpu.with_memory_space_constraint(array, pltpu.VMEM)


def edges_kernel(x_ref, u_ref, far_ref, x_rows, u_rows, sems):
    batch, rows, chans = x_ref.shape
    even = position()[0] == 0
    start = pl.multiple_of(jnp.where(even, 0, rows - 16), 16)
    copies = [
        pltpu.make_async_copy(src.at[:, pl.ds(start, 16), :], dst, sems.at[i])
        for i, (src, dst) in enumerate(((x_ref, x_rows), (u_ref, u_rows)))
    ]
    for copy in copies:
        copy.start()
    for copy in copies:
        copy.wait()
    for held, lo, hi in ((x_rows, 0, chans), (u_rows, chans, far_ref.shape[1])):
        wide = [held[b].astype(F32) for b in range(batch)]
        wide = jnp.concatenate([jnp.where(even, one[:2], one[14:]) for one in wide], axis=0)
        far_ref[:, lo:hi] = wide.astype(BF16)


def edges(x, u):
    batch, _, chans = x.shape
    feats = u.shape[2]
    return pl.pallas_call(
        edges_kernel,
        out_shape=shape((2 * batch, chans + feats), BF16),
        in_specs=[pl.BlockSpec(memory_space=pltpu.HBM)] * 2,
        out_specs=vmem(1)[0],
        scratch_shapes=[pltpu.VMEM((batch, 16, chans), BF16), pltpu.VMEM((batch, 16, feats), BF16),
                        pltpu.SemaphoreType.DMA((2,))],
        compiler_params=params(),
        cost_estimate=pl.CostEstimate(flops=0, bytes_accessed=1_000, transcendentals=0),
        name="edges",
    )(x, u)


def relay_kernel(far_ref, far_out):
    far_out[...] = far_ref[...]


def relay(far):
    return pl.pallas_call(
        relay_kernel,
        out_shape=shape(far.shape, BF16),
        in_specs=vmem(1),
        out_specs=vmem(1)[0],
        compiler_params=params(),
        cost_estimate=pl.CostEstimate(flops=10_000_000_000, bytes_accessed=1_000_000, transcendentals=0),
        name="relay",
    )(here(far))


def slope(w):
    w2 = w * w
    t = jnp.tanh(w * (w2 + KAPPA))
    return (1.0 + t) * (w * (w2 + KAPPA / 3.0) * (1.0 - t) + 1.0 / 3.0)


def tap_sets(taps):
    k_sum, k_dif, k_mid = 0.5 * (taps[0:1] + taps[2:3]), 0.5 * (taps[0:1] - taps[2:3]), taps[1:2]
    return (ALPHA * taps[0:1], ALPHA * taps[1:2], ALPHA * taps[2:3]), (0.75 * k_sum, 0.75 * k_dif, 0.75 * k_mid)


def products(scaled, value):
    return [tap * value for tap in scaled]


def slopes(before, centre, after, u):
    fwd = slope(centre[1] + before[0] + after[2])
    rev = slope(centre[1] + before[2] + after[0])
    return u * (fwd + rev), u * (fwd - rev)


def inner_gradients(j, proj, u_ref, k_ref, wide, out, gp_ref, gp_lane):
    batch, rows = u_ref.shape[:2]
    seg = rows // SUB
    pitch = seg + PAD
    lanes = slice(j * LANES, (j + 1) * LANES)
    scaled, (g_sum, g_dif, g_mid) = tap_sets(k_ref[:, lanes])
    for b in range(batch):
        for s in range(SUB):
            wide[b, s * pitch:s * pitch + seg] = u_ref[b, s * seg:(s + 1) * seg, lanes].astype(F32)
    for b in range(batch):
        def vector(i, b=b):
            return products(scaled, proj[j, b, pl.ds(i, SUB, stride=pitch), :])

        def put(i, before, centre, after, dif_before, dif_after, b=b):
            out[b, i * HOP:i * HOP + SUB, :] = (
                g_mid * centre + g_sum * (before + after) + g_dif * (dif_after - dif_before))

        head, tail = vector(0), vector(seg - 1)
        before, stop = [pltpu.roll(one, 1, 0) for one in tail], [pltpu.roll(one, SUB - 1, 0) for one in head]
        sums, difs = [], []
        centre = head
        for i in range(seg):
            after = stop if i == seg - 1 else (tail if i == seg - 2 else vector(i + 1))
            one, two = slopes(before, centre, after, wide[b, pl.ds(i, SUB, stride=pitch), :])
            sums.append(one)
            difs.append(two)
            before, centre = centre, after
            if i >= 2:
                put(i - 1, sums[i - 2], sums[i - 1], sums[i], difs[i - 2], difs[i])
        put(0, pltpu.roll(sums[-1], 1, 0), sums[0], sums[1], pltpu.roll(difs[-1], 1, 0), difs[1])
        put(seg - 1, sums[-2], sums[-1], pltpu.roll(sums[0], SUB - 1, 0), difs[-2], pltpu.roll(difs[0], SUB - 1, 0))
        done = jnp.concatenate(
            [out[b, pl.ds(lo * HOP + s, SUB, stride=HOP), :] for s in range(SUB) for lo in range(0, seg, SUB)], axis=0)
        gp_ref[b, :, gp_lane:gp_lane + LANES] = done.astype(BF16)


def project_kernel(x_ref, w_ref, u_ref, k_ref, proj, gp_ref, wide, out):
    batch, rows, _ = x_ref.shape
    seg = rows // SUB
    pitch = seg + PAD
    tiles = gp_ref.shape[2] // LANES
    for b in range(batch):
        body = jnp.dot(x_ref[b], w_ref[...], preferred_element_type=F32).astype(BF16).astype(F32)
        for j in range(proj.shape[0]):
            for s in range(SUB):
                proj[j, b, s * pitch:s * pitch + seg] = body[s * seg:(s + 1) * seg, j * LANES:(j + 1) * LANES]
    for j in range(tiles):
        inner_gradients(j, proj, u_ref, k_ref, wide, out, gp_ref, j * LANES)


def pitched(rows):
    seg = rows // SUB
    return SUB * (seg + PAD) + seg


def sample_scratch(batch, rows):
    return [pltpu.VMEM((batch, pitched(rows), LANES), F32), pltpu.VMEM((batch, rows // SUB * HOP + 2 * SUB, LANES), F32)]


def project(x, w, u, k, ncol):
    batch, rows, _ = x.shape
    feats = w.shape[1]
    return pl.pallas_call(
        project_kernel,
        out_shape=[shape((feats // LANES, batch, pitched(rows), LANES), F32), shape((batch, rows, ncol), BF16)],
        in_specs=vmem(4),
        out_specs=vmem(2),
        scratch_shapes=sample_scratch(batch, rows),
        compiler_params=params(),
        cost_estimate=pl.CostEstimate(flops=4_000_000_000, bytes_accessed=4_000_000, transcendentals=0),
        name="project",
    )(*map(here, (x, w, u, k)))


def around(low, high):
    return jnp.concatenate([low, jnp.zeros((SUB - 4, low.shape[1]), low.dtype), high], axis=0)


def halo_of(pair_ref, far_rows):
    batch, rows, _ = pair_ref.shape
    even = position()[0] == 0
    far_rows = far_rows.astype(F32)
    result = []
    for b in range(batch):
        far = far_rows[2 * b:2 * b + 2]
        low, high = pair_ref[b, rows - 16:rows].astype(F32)[14:], pair_ref[b, 0:16].astype(F32)[:2]
        result.append(around(jnp.where(even, far, low), jnp.where(even, high, far)))
    return result


def finish(j, proj, u_ref, k_ref, halo_p, halo_u, inner_ref, gp_ref, gp_lane, gpt):
    batch, rows = u_ref.shape[:2]
    seg = rows // SUB
    pitch = seg + PAD
    lanes = slice(j * LANES, (j + 1) * LANES)
    cols = slice(gp_lane, gp_lane + LANES)
    scaled, (g_sum, g_dif, g_mid) = tap_sets(k_ref[:, lanes])
    sub = lax.broadcasted_iota(jnp.int32, (SUB, LANES), 0)

    def centred(low, high, halo):
        ends = jnp.where(sub == 0, pltpu.roll(halo, SUB - 1, 0), pltpu.roll(halo, 1, 0))
        inside = jnp.where(sub < 4, pltpu.roll(low, 1, 0), pltpu.roll(high, SUB - 1, 0))
        return jnp.where(jnp.logical_or(sub == 0, sub == SUB - 1), ends, inside)

    for b in range(batch):
        low = proj[j, b, 0:SUB]
        high = proj[j, b, (SUB - 1) * pitch + seg - SUB:(SUB - 1) * pitch + seg]
        halo = halo_p[b][:, lanes]
        before = jnp.where(sub < 2, halo, jnp.where(sub < 4, pltpu.roll(low, 2, 0), high))
        after = jnp.where(sub < 4, low, jnp.where(sub < 6, pltpu.roll(high, SUB - 2, 0), halo))
        u_low = u_ref[b, 0:16, lanes].astype(F32)[:SUB]
        u_high = u_ref[b, rows - 16:rows, lanes].astype(F32)[16 - SUB:]
        u = centred(u_low, u_high, halo_u[b][:, lanes])
        sums, difs = slopes(*(products(scaled, one) for one in (before, centred(low, high, halo), after)), u)
        ends = (g_mid * sums + g_sum * (pltpu.roll(sums, 1, 0) + pltpu.roll(sums, SUB - 1, 0))
                + g_dif * (pltpu.roll(difs, SUB - 1, 0) - pltpu.roll(difs, 1, 0)))
        first = inner_ref[b, 0:16, cols].astype(F32)
        last_rows = inner_ref[b, rows - 16:rows, cols].astype(F32)
        first = jnp.concatenate([jnp.where(sub < 2, pltpu.roll(ends, SUB - 1, 0), first[:SUB]), first[SUB:]], axis=0)
        last_rows = jnp.concatenate(
            [last_rows[:SUB], jnp.where(sub >= 6, pltpu.roll(ends, 1, 0), last_rows[SUB:])], axis=0)
        gp_ref[b, 0:16, cols] = first.astype(BF16)
        gp_ref[b, rows - 16:rows, cols] = last_rows.astype(BF16)
        if inner_ref is not gp_ref:
            gp_ref[b, 16:rows - 16, cols] = inner_ref[b, 16:rows - 16, cols]
        gpt[cols, b * rows:(b + 1) * rows] = gp_ref[b, :, cols].T


def hand_out(core, gpt, mine_ref, send_ref):
    strip = mine_ref.shape[1]
    for z in range(mine_ref.shape[0]):
        for result, who in ((mine_ref, core), (send_ref, 1 - core)):
            result[z] = gpt[pl.ds(pl.multiple_of((2 * z + who) * strip, 16), strip), :]


def early_kernel(
    x_ref, w_ref, u_ref, k_ref, pair_x, pair_u, far_ref, proj, inner_ref,
    gp_ref, halo_ref, halo_u_ref, *rest,
):
    *parts, gpt = rest
    batch, rows, chans = x_ref.shape
    halo_x = halo_of(pair_x, far_ref[:, :chans])
    halo_u = halo_of(pair_u, far_ref[:, chans:])
    for b in range(batch):
        halo_u_ref[b] = halo_u[b]
    halo_x = jnp.concatenate(halo_x, axis=0).astype(BF16)
    halo_all = jnp.dot(halo_x, w_ref[...], preferred_element_type=F32).astype(BF16).astype(F32)
    for b in range(batch):
        halo_ref[b] = halo_all[b * SUB:(b + 1) * SUB]
    halo_p = [halo_all[b * SUB:(b + 1) * SUB] for b in range(batch)]
    for j in range(gp_ref.shape[2] // LANES):
        finish(j, proj, u_ref, k_ref, halo_p, halo_u, inner_ref, gp_ref, j * LANES, gpt)
    if parts:
        hand_out(position()[0], gpt, *parts)


def late_kernel(
    col, u_ref, k_ref, proj, halo_ref, halo_u_ref,
    gp_ref, mine_ref, send_ref, wide, out, gpt,
):
    batch, rows, feats = u_ref.shape
    halo_u = [halo_u_ref[b] for b in range(batch)]
    halo_p = [halo_ref[b] for b in range(batch)]
    for t in range(gp_ref.shape[2] // LANES):
        j = col // LANES + t
        inner_gradients(j, proj, u_ref, k_ref, wide, out, gp_ref, t * LANES)
        finish(j, proj, u_ref, k_ref, halo_p, halo_u, gp_ref, gp_ref, t * LANES, gpt)
    hand_out(position()[0], gpt, mine_ref, send_ref)


def early(x, w, u, k, pair_x, pair_u, far, proj, inner, strips, strip):
    batch, rows, _ = x.shape
    ncol = inner.shape[2]
    parts = [shape((strips, strip, batch * rows), BF16)] * 2 if strips else []
    return pl.pallas_call(
        early_kernel,
        out_shape=[shape(inner.shape, BF16)] + [shape((batch, SUB, w.shape[1]), F32)] * 2 + parts,
        in_specs=vmem(9),
        out_specs=vmem(3 + len(parts)),
        scratch_shapes=[pltpu.VMEM((ncol, batch * rows), BF16)],
        compiler_params=params(),
        cost_estimate=pl.CostEstimate(flops=1_000_000_000, bytes_accessed=4_000_000, transcendentals=0),
        name="early",
    )(*map(here, (x, w, u, k, pair_x, pair_u, far, proj, inner)))


def late(u, k, proj, halo, halo_u, col, ncol, strips, strip):
    batch, rows, _ = u.shape
    part = shape((strips, strip, batch * rows), BF16)
    return pl.pallas_call(
        functools.partial(late_kernel, col),
        out_shape=[shape((batch, rows, ncol), BF16), part, part],
        in_specs=vmem(5),
        out_specs=vmem(3),
        scratch_shapes=sample_scratch(batch, rows) + [pltpu.VMEM((ncol, batch * rows), BF16)],
        compiler_params=params(),
        cost_estimate=pl.CostEstimate(flops=4_000_000_000, bytes_accessed=4_000_000, transcendentals=0),
        name="late",
    )(*map(here, (u, k, proj, halo, halo_u)))


def stacked(ref):
    return ref[...].reshape(ref.shape[0] * ref.shape[1], ref.shape[2])


def place_blocks(strips, sums_ref, out_ref):
    core, zed, dee = position()
    strip = sums_ref.shape[1]
    half = strip // 2
    left = lax.broadcasted_iota(jnp.int32, (half, LANES), 1) < LANES // 2

    def slot(turn, turns):
        return sum(jnp.where(turn == one, at, 0) for at, one in enumerate(turns))

    for z in strips:
        z_slot = slot(jnp.bitwise_xor(zed, z), [pair[1] for pair in FIRST])
        for b in range(4):
            b_slot = slot(jnp.bitwise_xor(dee, b), [pair[0] for pair in FIRST])
            at, spot = jnp.where(core == 0, b_slot, z_slot), jnp.where(core == 0, z, b)
            full = (3 * (b // 2) + 2 * (b % 2)) * LANES
            rest = (3 * (b // 2) + 1) * LANES
            top, bottom = sums_ref[z, 0:half, rest:rest + LANES], sums_ref[z, half:strip, rest:rest + LANES]
            if b % 2 == 0:
                packed = jnp.where(left, top, pltpu.roll(bottom, LANES // 2, 1))
            else:
                packed = jnp.where(left, pltpu.roll(top, LANES // 2, 1), bottom)
            out_ref[at, spot, 0:strip] = sums_ref[z, :, full:full + LANES].astype(BF16)
            out_ref[at, spot, strip:strip + half] = packed.astype(BF16)


def own_kernel(x_ref, other_ref, mine_a, mine_b, got_a, sums_ref, out_ref):
    flat, other = stacked(x_ref), stacked(other_ref)
    half, strip, _ = mine_a.shape
    later = jnp.dot(stacked(mine_b), flat, preferred_element_type=F32)
    sooner = (jnp.dot(stacked(mine_a), flat, preferred_element_type=F32)
              + jnp.dot(stacked(got_a), other, preferred_element_type=F32))
    for z in range(half):
        sums_ref[half + z] = later[z * strip:(z + 1) * strip]
        sums_ref[z] = sooner[z * strip:(z + 1) * strip]
    place_blocks(range(half), sums_ref, out_ref)


def own(x, other, mine_a, mine_b, got_a):
    half, strip, _ = mine_a.shape
    return pl.pallas_call(
        own_kernel,
        out_shape=[shape((2 * half, strip, x.shape[2]), F32), shape((4, 4, strip + strip // 2, LANES), BF16)],
        in_specs=vmem(5),
        out_specs=vmem(2),
        compiler_params=params(),
        cost_estimate=pl.CostEstimate(flops=1_000_000_000, bytes_accessed=4_000_000, transcendentals=0),
        name="own",
    )(*map(here, (x, other, mine_a, mine_b, got_a)))


def pack_kernel(other_ref, got_b, sums_in, blocks_in, sums_ref, out_ref):
    half, strip, _ = got_b.shape
    later = jnp.dot(stacked(got_b), stacked(other_ref), preferred_element_type=F32)
    for z in range(half):
        sums_ref[half + z] = sums_in[half + z] + later[z * strip:(z + 1) * strip]
    place_blocks(range(half, 2 * half), sums_ref, out_ref)


def pack(other, got_b, sums, blocks):
    return pl.pallas_call(
        pack_kernel,
        out_shape=[shape(sums.shape, F32), shape(blocks.shape, BF16)],
        in_specs=vmem(4),
        out_specs=vmem(2),
        input_output_aliases={2: 0, 3: 1},
        compiler_params=params(),
        name="pack",
    )(*map(here, (other, got_b, sums, blocks)))[1]


def fold_kernel(own_ref, one_ref, two_ref, three_ref, token, *outs):
    core, zed, dee = position()
    mine = jnp.where(core == 0, zed, dee)
    for k in (3, 2, 1, 0):
        j = jnp.bitwise_xor(mine, k)
        total = own_ref[0, j].astype(F32) + one_ref[j].astype(F32) + two_ref[j].astype(F32) + three_ref[j].astype(F32)
        outs[k][...] = total.astype(outs[k].dtype)


def fold(parts, token):
    block = parts[1].shape[1:]
    return pl.pallas_call(
        fold_kernel,
        out_shape=[shape(block, F32)] + [shape(block, BF16)] * 3,
        in_specs=vmem(5),
        out_specs=vmem(4),
        compiler_params=params(),
        name="fold",
    )(*map(here, parts), here(token))


def input_kernel(gp_a, gp_b, w_ref, out_ref, token):
    token[...] = jnp.zeros_like(token)
    cut = gp_a.shape[2]
    for b in range(out_ref.shape[0]):
        total = lax.dot_general(gp_a[b], w_ref[:, :cut], (((1,), (1,)), ((), ())), preferred_element_type=F32)
        total += lax.dot_general(gp_b[b], w_ref[:, cut:], (((1,), (1,)), ((), ())), preferred_element_type=F32)
        out_ref[b] = total.astype(BF16)


def input_gradient(gp_a, gp_b, w):
    batch, rows, _ = gp_a.shape
    return pl.pallas_call(
        input_kernel,
        out_shape=[jax.ShapeDtypeStruct((batch, rows, w.shape[0]), BF16), shape((SUB, LANES), F32)],
        in_specs=vmem(3),
        out_specs=vmem(2),
        compiler_params=params(),
        cost_estimate=pl.CostEstimate(flops=2_000_000_000, bytes_accessed=1_000_000, transcendentals=0),
        name="input_gradient",
    )(here(gp_a), here(gp_b), here(w))


def last_kernel(scale, own_ref, one_ref, two_ref, three_ref, out_ref):
    odd = lax.rem(position()[2], 2)
    total = own_ref[...] + one_ref[...].astype(F32) + two_ref[...].astype(F32) + three_ref[...].astype(F32)
    total = total * scale
    strip = out_ref.shape[0]
    half = LANES // 2
    full, rest = total[:strip], total[strip:]
    rest = jnp.concatenate([rest[:, :half], rest[:, half:]], axis=0)

    @pl.when(odd == 0)
    def _():
        out_ref[:, :LANES] = full
        out_ref[:, LANES:] = rest

    @pl.when(odd == 1)
    def _():
        out_ref[:, :half] = rest
        out_ref[:, half:] = full


def last(parts, scale):
    strip = parts[0].shape[0] * 2 // 3
    return pl.pallas_call(
        functools.partial(last_kernel, scale),
        out_shape=jax.ShapeDtypeStruct((strip, LANES + LANES // 2), F32),
        in_specs=vmem(4),
        out_specs=vmem(1)[0],
        compiler_params=params(),
        name="last",
    )(*parts).T


def near_pairs():
    count = lax.axis_size("seq")
    return [(i, i ^ 1) for i in range(count) if i ^ 1 < count]


def far_pairs():
    count = lax.axis_size("seq")
    pairs = [(i, i - 1 if i % 2 == 0 else i + 1) for i in range(count)]
    return [(a, b) for a, b in pairs if 0 <= b < count]


def exchange(array, one, two):
    n_seq, n_dp = lax.axis_size("seq"), lax.axis_size("dp")
    pairs = [(i, i ^ (two if (i // n_dp) % 2 else one)) for i in range(n_seq * n_dp)]
    return lax.ppermute(array, ("seq", "dp"), pairs)


def spread(x, w, u, k, pair_x, pair_u, far):
    batch = x.shape[0]
    proj, inner = project(x, w, u, k, w.shape[1])
    gp, *_ = early(x, w, u, k, pair_x, pair_u, far, proj, inner, 0, 0)
    input_grad = jnp.einsum("bpf,cf->bpc", gp, w, preferred_element_type=F32).astype(BF16)
    partial = lax.dot_general(x, gp, (((0, 1), (0, 1)), ((), ())), preferred_element_type=F32)
    over_seq = lax.psum_scatter(partial, "seq", scatter_dimension=1, tiled=True)
    total = lax.psum_scatter(over_seq, "dp", scatter_dimension=0, tiled=True)
    return input_grad, total / (batch * lax.axis_size("dp"))


def on_device(skip_input, upstream, proj_weight, depth_kernel):
    batch, rows, chans = skip_input.shape
    feats = upstream.shape[2]
    n_seq, n_dp = lax.axis_size("seq"), lax.axis_size("dp")
    seq, dee = lax.axis_index("seq"), lax.axis_index("dp")
    core, zed = seq % 2, seq // 2
    strip = feats // n_seq
    strips = n_seq // 4
    ncol = feats // 2

    there = functools.partial(pltpu.with_memory_space_constraint, memory_space=pltpu.HBM)
    x, w, u, k = skip_input, proj_weight, upstream, depth_kernel
    pair_x = lax.ppermute(x, "seq", near_pairs())
    pair_u = lax.ppermute(u, "seq", near_pairs())
    far = lax.ppermute(relay(edges(there(x), there(u))), "seq", far_pairs())
    if n_seq != 8 or n_dp != 4 or chans != 4 * (LANES + LANES // 2):
        return spread(x, w, u, k, pair_x, pair_u, far)
    proj, inner = project(x, w, u, k, ncol)
    gp_a, halo, halo_u, mine_a, send_a = early(x, w, u, k, pair_x, pair_u, far, proj, inner, strips, strip)
    got_a = lax.ppermute(send_a, "seq", near_pairs())
    gp_b, mine_b, send_b = late(u, k, proj, halo, halo_u, ncol, feats - ncol, strips, strip)
    got_b = lax.ppermute(send_b, "seq", near_pairs())
    blocks = pack(pair_x, got_b, *own(x, pair_x, mine_a, mine_b, got_a))

    input_grad, token = input_gradient(gp_a, gp_b, w)
    z_bits = [m * 2 * n_dp for m in range(4)]
    got = [exchange(blocks[i], *(FIRST[i][0], z_bits[FIRST[i][1]])) for i in (3, 2, 1)]
    own_block, *messages = fold([blocks] + got, token)
    got = [exchange(messages[k - 1], z_bits[k], k) for k in (3, 2, 1)]
    return input_grad, last([own_block] + got, 1.0 / (batch * n_dp))


def solution(mesh):
    return jax.shard_map(
        on_device,
        mesh=mesh,
        in_specs=(P("dp", "seq", None), P("dp", "seq", None), P(), P()),
        out_specs=(P("dp", "seq", None), P("dp", "seq")),
        check_vma=False,
    )
```
